32 devices in a mesh: sea: 2 (over y), tm: 16 (over z, x, core).
Axes of the slice: x: 2, y: 2, z: 4, core: 2. Of those that a mesh axis runs over, the one named last changes fastest.
Arguments:
- wet_station: int32 [16384, 128], P(('sea', 'tm')), parts along dimension 0, may hold values from 0 to 99
- wet_girth: int32 [16384, 128], P(('sea', 'tm')), parts along dimension 0, may hold values from 0 to 499
- wet_count: int32 [16384], P(('sea', 'tm')), parts along dimension 0, may hold values from 1 to 128, as said below
- pressure: bfloat16 [16384, 128], P(('sea', 'tm')), parts along dimension 0, may hold values from -6 to 6
- panel_area: float32 [50000], replicated, may hold values from 0.2 to 2
- panel_patch: int32 [50000], replicated, may hold values from 0 to 3071
- patch_modes: bfloat16 [3072, 64], replicated, may hold values from -0.75 to 0.75
- impulse: bfloat16 [512, 64, 64], replicated, may hold values from -0.03125 to 0.03125
- stress_map: bfloat16 [64, 128], P(None, 'tm'), may hold values from -0.75 to 0.75
Outputs:
- stress: bfloat16 [128, 16384], P('tm', 'sea'), parts along dimension 1
The draws below stay inside these ranges and needn't reach their ends.
There are 2 independent parts, one for each index of `sea`. The reference program is written for one: setup_inputs(seed, part) draws one part's arguments, and reference() takes and returns one part's arrays. A program takes and returns all parts, laid end to end along the dimension named above; an argument that names none is the same for every part. Nothing has to cross between parts.
Inputs may be any that keep to these rules, and one draw needn't show every extreme that they name: `wet_count`: every time step has at least one live slot, and some time step of every draw lists 128 live slots.
All inputs are finite; a program needn't handle non-finite values.
Results may differ from the reference program's by a relative error of at most 0.0058.
Values may be sent and summed in bfloat16 or wider, within the bound.
No kernel may reach another device: no remote copies, remote signals or barrier semaphores. Data moves between devices by JAX's collectives and lax.ppermute only.
A program may use at most 64 MiB of HBM per device.

```python
import math
import jax
import jax.numpy as jnp
from jax import lax

STATIONS = 100
GIRTH = 500
PANELS = 50000
PATCHES = 3072
MODES = 64
LAGS = 512
WMAX = 128
T_DEV = 512
TIME = 8192
HOT = 128


def draw_wet_count(key, part):
    first_key, second_key = jax.random.split(jax.random.fold_in(key, 7))
    counts = jax.random.randint(first_key, (TIME,), 1, WMAX + 1, dtype=jnp.int32)
    filled = jax.random.randint(second_key, (), 0, TIME, dtype=jnp.int32)
    return counts.at[filled].set(WMAX)


def touch_ends(drawn, stream_key, least, high):
    shape = drawn.shape
    place = [jax.random.randint(jax.random.fold_in(stream_key, axis), (), 0, shape[axis]) for axis in range(len(shape))]
    drawn = drawn.at[tuple(place)].set(least)
    longest = shape.index(max(shape))
    place[longest] = (place[longest] + 1) % shape[longest]
    return drawn.at[tuple(place)].set(high)


def block_scale(key, dims, cuts, low, largest):
    def one(dim, blocks):
        steps = jax.random.uniform(jax.random.fold_in(jax.random.fold_in(key, 6), dim), (blocks,), jnp.float32, low / len(cuts), largest / len(cuts))
        return jnp.repeat(jnp.exp(steps), dims[dim] // blocks).reshape((-1,) + (1,) * (len(dims) - dim - 1))

    factor_of = one(*cuts[0])
    for cut in cuts[1:]:
        factor_of = factor_of * one(*cut)
    return factor_of


def centred(key, dims, width, bound, shards=(), held_as=jnp.bfloat16):
    array = jax.random.normal(key, dims, jnp.float32) * width
    if len(shards) > 0:
        array = block_scale(key, dims, shards, -0.22, 0.18) * array
    return jnp.clip(array, min=-bound, max=bound).astype(held_as)


def setup_inputs(seed: int = 0, part: int = 0) -> dict:
    key_of = jax.random.split(jax.random.key(seed), 10)
    part_keys = jax.random.split(jax.random.fold_in(key_of[9], part), 10)
    return {
        "wet_station": touch_ends(jax.random.randint(part_keys[0], (TIME, WMAX), 0, STATIONS), jax.random.fold_in(part_keys[0], 1), 0, STATIONS - 1).astype(jnp.int32),
        "wet_girth": touch_ends(jax.random.randint(part_keys[1], (TIME, WMAX), 0, GIRTH), jax.random.fold_in(part_keys[1], 1), 0, GIRTH - 1).astype(jnp.int32),
        "wet_count": draw_wet_count(jax.random.fold_in(jax.random.fold_in(key_of[9], part), 71), part),
        "pressure": centred(part_keys[3], (TIME, WMAX), 1.0, 6.0, ((0, 16),)),
        "panel_area": jnp.clip(jnp.exp(jax.random.uniform(key_of[4], (PANELS,), jnp.float32, math.log(0.2), math.log(2.0))), 0.2, 2.0),
        "panel_patch": touch_ends(jax.random.randint(key_of[5], (PANELS,), 0, PATCHES), jax.random.fold_in(key_of[5], 1), 0, PATCHES - 1).astype(jnp.int32),
        "patch_modes": centred(key_of[6], (PATCHES, MODES), (WMAX // 2) ** -0.5, 0.75),
        "impulse": centred(key_of[7], (LAGS, MODES, MODES), (LAGS * MODES) ** -0.5, 0.03125),
        "stress_map": centred(key_of[8], (MODES, HOT), MODES ** -0.5, 0.75, ((1, 16),)),
    }


def block_forcing(block, panel_area, panel_patch, patch_modes):
    stations, girths, counts, press = block
    slots = stations.shape[1]
    panels = (stations * GIRTH + girths).astype(jnp.int32)
    area = panel_area[panels]
    patch = panel_patch[panels]
    live = jnp.arange(slots, dtype=jnp.int32)[None, :] < counts[:, None]
    force = jnp.where(live, press.astype(jnp.float32) * area, jnp.float32(0.0))
    mode_rows = patch_modes[patch].astype(jnp.float32)
    return jnp.einsum("tk,tkm->tm", force, mode_rows, precision=lax.Precision.HIGHEST)


def reference(wet_station, wet_girth, wet_count, pressure, panel_area, panel_patch, patch_modes, impulse, stress_map):
    rows_block = min(64, T_DEV)
    blocks_all = TIME // rows_block
    blocks = (wet_station.reshape(blocks_all, rows_block, WMAX), wet_girth.reshape(blocks_all, rows_block, WMAX), wet_count.reshape(blocks_all, rows_block), pressure.reshape(blocks_all, rows_block, WMAX))
    forcing = lax.map(lambda b: block_forcing(b, panel_area, panel_patch, patch_modes), blocks)
    forcing = forcing.reshape(TIME, MODES).astype(jnp.bfloat16)
    extended = jnp.concatenate([jnp.zeros((LAGS - 1, MODES), jnp.bfloat16), forcing], 0)
    response = lax.conv_general_dilated(extended[None], impulse[::-1], (1,), "VALID", dimension_numbers=("NWC", "WIO", "NWC"), preferred_element_type=jnp.float32)[0]
    response = response.astype(jnp.bfloat16)
    stress = lax.dot_general(stress_map, response, (((0,), (1,)), ((), ())), preferred_element_type=jnp.float32)
    return stress.astype(jnp.bfloat16)
```

```python
import functools

import jax
import jax.numpy as jnp
from jax import lax
from jax.experimental import pallas as pl
from jax.experimental.pallas import tpu as pltpu
from jax.sharding import PartitionSpec as P

F32, BF16, I32 = jnp.float32, jnp.bfloat16, jnp.int32
GIRTH = 500
LANES = 128
HALF = 200
AREA_SCALE = 32767.0


def pow2_up(x, e, bits):
    for b in range(bits):
        x = jnp.where((e & (1 << b)) != 0, x * float(2 ** (1 << b)), x)
    return x


def pow2_down(x, bits, top):
    e = jnp.zeros(x.shape, I32)
    for b in reversed(range(bits)):
        big = x >= float(top * 2 ** ((1 << b)))
        x = jnp.where(big, x * float(2.0 ** -(1 << b)), x)
        e = e + jnp.where(big, jnp.int32(1 << b), jnp.int32(0))
    return x, e


def forcing_kernel(st_any, gi_any, cnt_any, pr_any, first_ref, second_ref, modes_any, out_ref,
                   st_ref, gi_ref, cnt_ref, pr_ref, modes_ref, sems, tab, live, rowv, colv, sel1, sel2, fv, hiv, lov, wbuf, *, group):
    steps = st_ref.shape[0]
    copies = [pltpu.make_async_copy(a, b, sems.at[i]) for i, (a, b) in enumerate((
        (st_any, st_ref), (gi_any, gi_ref), (cnt_any, cnt_ref), (pr_any, pr_ref), (modes_any, modes_ref)))]
    for c in copies:
        c.start()
    for h in range(2):
        for part, ref in enumerate((first_ref, second_ref)):
            tab[HALF * part:HALF * (part + 1), LANES * h:LANES * (h + 1)] = ref[HALF * h:HALF * (h + 1), :]
    for c in copies:
        c.wait()
    slot = lax.broadcasted_iota(I32, (LANES, LANES), 1).astype(F32)
    counts = cnt_ref[...].astype(F32)
    for j in range(steps // LANES):
        per_step = jnp.broadcast_to(counts[j:j + 1, :], (LANES, LANES)).T
        here = slice(LANES * j, LANES * (j + 1))
        live[here, :] = jnp.where(slot < per_step, pr_ref[here, :].astype(F32), 0.0)
    panel = st_ref[...] * GIRTH + gi_ref[...]
    hi = panel >> 7
    second = hi >= HALF
    rowv[...] = jnp.where(second, hi - HALF, hi)
    colv[...] = ((panel & 127) + jnp.where(second, LANES, 0)).astype(F32)

    n_groups = steps // group
    sub = lax.broadcasted_iota(I32, (8, LANES), 0)
    iota_b = lax.broadcasted_iota(I32, (256, LANES), 0).astype(F32).astype(BF16)
    iota16 = lax.broadcasted_iota(I32, (16, LANES), 0)
    one = jnp.ones((), BF16)
    zero = jnp.zeros((), BF16)

    def onehot(row_f32):
        b = jnp.broadcast_to(row_f32, (256, LANES)).astype(BF16)
        return jnp.where(iota_b == b, one, zero)

    def stage1(base):
        for p in range(group // 2):
            t0 = base + 2 * p
            oh = jnp.concatenate([onehot(colv[pl.ds(t0, 1), :]), onehot(colv[pl.ds(t0 + 1, 1), :])], axis=1)
            r = jnp.dot(tab[...], oh, preferred_element_type=F32)
            for j in range(2):
                want = jnp.broadcast_to(rowv[pl.ds(t0 + j, 1), :], (8, LANES)) - sub
                a1 = jnp.zeros((8, LANES), F32)
                a2 = jnp.zeros((8, LANES), F32)
                for v in range(HALF // 8):
                    hit = want == 8 * v
                    a1 = jnp.where(hit, r[8 * v:8 * v + 8, LANES * j:LANES * (j + 1)], a1)
                    a2 = jnp.where(hit, r[HALF + 8 * v:HALF + 8 * v + 8, LANES * j:LANES * (j + 1)], a2)
                sel1[pl.ds(t0 + j, 1), :] = jnp.sum(a1, axis=0, keepdims=True)
                sel2[pl.ds(t0 + j, 1), :] = jnp.sum(a2, axis=0, keepdims=True)

    def decode(base):
        x1 = sel1[pl.ds(base, group), :]
        x2 = sel2[pl.ds(base, group), :]
        m1, e1 = pow2_down(jnp.abs(x1), 6, 128)
        m2, e2 = pow2_down(jnp.abs(x2), 6, 128)
        qi = (m1.astype(I32) - 128) + (e1 << 7) + jnp.where(x1 < 0, 1 << 13, 0) + jnp.where(x2 < 0, 1 << 14, 0) + ((e2 & 1) << 15)
        area = qi.astype(F32) * (1.0 / AREA_SCALE)
        pa = e2 >> 1
        lov[pl.ds(base, group), :] = (m2 - 128.0) + ((pa & 1) << 7).astype(F32)
        hiv[pl.ds(base, group), :] = pa >> 1
        fv[pl.ds(base, group), :] = live[pl.ds(base, group), :] * area

    def stage2(base):
        for p in range(group // 2):
            t0 = base + 2 * p
            oh = jnp.concatenate([onehot(lov[pl.ds(t0, 1), :]), onehot(lov[pl.ds(t0 + 1, 1), :])], axis=1)
            rows = []
            zer = jnp.zeros((16, LANES), BF16)
            for j in range(2):
                f = jnp.broadcast_to(fv[pl.ds(t0 + j, 1), :], (16, LANES))
                hit = jnp.broadcast_to(hiv[pl.ds(t0 + j, 1), :], (16, LANES)) == iota16
                fm = jnp.where(hit, f, 0.0)
                fh = fm.astype(BF16)
                fl = (fm - fh.astype(F32)).astype(BF16)
                for part in (fh, fl):
                    rows.append(jnp.concatenate([part, zer] if j == 0 else [zer, part], axis=1))
            a = jnp.concatenate(rows, axis=0)
            w = lax.dot_general(a, oh, (((1,), (1,)), ((), ())), preferred_element_type=F32)
            for j in range(2):
                both = w[32 * j:32 * j + 16] + w[32 * j + 16:32 * j + 32]
                for c in range(2):
                    wbuf[c, pl.ds((t0 + j) * 16, 16), :] = both[:, LANES * c:LANES * (c + 1)]

    stage1(0)
    decode(0)

    def loop(g, c):
        base = pl.multiple_of(g * group, group)
        stage1(base + group)
        stage2(base)
        decode(base + group)
        return c

    lax.fori_loop(0, n_groups - 1, loop, 0)
    stage2((n_groups - 1) * group)

    acc = jnp.zeros((steps, modes_ref.shape[0]), F32)
    for h in range(modes_ref.shape[1] // 256):
        m = modes_ref[:, 256 * h:256 * h + 256]
        w = jnp.concatenate([wbuf.at[c][pl.ds(h, steps, 16), :] for c in range(2)], axis=1)
        wh = w.astype(BF16)
        wl = (w - wh.astype(F32)).astype(BF16)
        acc = acc + lax.dot_general(wh, m, (((1,), (1,)), ((), ())), preferred_element_type=F32)
        acc = acc + lax.dot_general(wl, m, (((1,), (1,)), ((), ())), preferred_element_type=F32)
    out_ref[...] = acc.astype(BF16)


def whole(shape):
    return pl.BlockSpec(shape, lambda i: (0,) * len(shape))


def encoded(panel_area, panel_patch):
    pad = 2 * HALF * LANES - panel_area.shape[0]
    q = (jnp.pad(panel_area, (0, pad)) * AREA_SCALE + 0.5).astype(I32)
    patch = jnp.pad(panel_patch, (0, pad))
    first = pow2_up(((q & 127) + 128).astype(F32), (q >> 7) & 63, 6)
    first = jnp.where(((q >> 13) & 1) == 1, -first, first).astype(BF16)
    second = pow2_up(((patch & 127) + 128).astype(F32), (patch >> 7) * 2 + (q >> 15), 6)
    second = jnp.where(((q >> 14) & 1) == 1, -second, second).astype(BF16)
    return first.reshape(2 * HALF, LANES), second.reshape(2 * HALF, LANES)


def forcing(wet_station, wet_girth, wet_count, pressure, panel_area, panel_patch, patch_modes, group=32):
    steps = wet_station.shape[0]
    modes = patch_modes.shape[1]
    first, second = encoded(panel_area, panel_patch)
    args = (wet_station, wet_girth, wet_count.reshape(steps // LANES, LANES), pressure, first, second, patch_modes.T)
    return pl.pallas_call(
        functools.partial(forcing_kernel, group=group),
        out_shape=jax.ShapeDtypeStruct((steps, modes), BF16),
        in_specs=[pl.BlockSpec(memory_space=pltpu.VMEM if i in (4, 5) else pltpu.HBM) for i in range(len(args))],
        out_specs=pl.BlockSpec(memory_space=pltpu.VMEM),
        scratch_shapes=[
            *[pltpu.VMEM(args[i].shape, args[i].dtype) for i in (0, 1, 2, 3, 6)],
            pltpu.SemaphoreType.DMA((5,)),
            pltpu.VMEM((2 * HALF, 256), BF16), pltpu.VMEM((steps, LANES), F32),
            pltpu.VMEM((steps, LANES), I32), pltpu.VMEM((steps, LANES), F32),
            pltpu.VMEM((steps, LANES), F32), pltpu.VMEM((steps, LANES), F32),
            pltpu.VMEM((steps, LANES), F32), pltpu.VMEM((steps, LANES), I32), pltpu.VMEM((steps, LANES), F32),
            pltpu.VMEM((2, steps * 16, LANES), F32),
        ],
        compiler_params=pltpu.CompilerParams(vmem_limit_bytes=16 * 1024 * 1024),
        cost_estimate=pl.CostEstimate(flops=2 * 10 ** 10, bytes_accessed=2 * 10 ** 6, transcendentals=0),
        name="forcing",
    )(*args)


def weights_kernel(imp_ref, out_ref, turned):
    modes = out_ref.shape[1] // 4
    quarter = imp_ref.shape[1] // 4

    def turn(m, carry):
        rows = imp_ref[pl.ds(pl.multiple_of(m * modes, modes), modes), :]
        for h in range(2):
            q = 2 * h * quarter
            block = jnp.concatenate([rows[:, q:q + quarter], rows[:, q + quarter:q + 2 * quarter]], axis=0)
            turned[h, pl.ds(pl.multiple_of(m * quarter, quarter), quarter), :] = block.astype(F32).T
        return carry

    lax.fori_loop(0, modes, turn, 0, unroll=4)

    def gather(r, carry):
        lines = [turned.at[h][pl.ds(r, modes, quarter), :].astype(BF16) for h in range(2)]
        out_ref[pl.ds(pl.multiple_of(r * modes, modes), modes), :] = jnp.concatenate(lines, axis=1)
        return carry

    lax.fori_loop(0, quarter, gather, 0, unroll=4)


def impulse_weights(impulse):
    lags, modes, _ = impulse.shape
    flat = jnp.transpose(impulse, (1, 2, 0)).reshape(modes * modes, lags)
    rows = lags // 4 * modes
    return pl.pallas_call(
        weights_kernel,
        out_shape=jax.ShapeDtypeStruct((rows, 4 * modes), BF16),
        in_specs=[pl.BlockSpec(memory_space=pltpu.VMEM)],
        out_specs=pl.BlockSpec(memory_space=pltpu.VMEM),
        scratch_shapes=[pltpu.VMEM((2, rows, 2 * modes), F32)],
        compiler_params=pltpu.CompilerParams(vmem_limit_bytes=12 * 1024 * 1024),
        cost_estimate=pl.CostEstimate(flops=10 ** 9, bytes_accessed=8 * 10 ** 6, transcendentals=0),
        name="impulse_weights",
    )(flat)


def response_kernel(early_ref, force_ref, weights, map_ref, out_ref, pair, shifts, acc):
    steps, modes = force_ref.shape
    quarter = weights.shape[0] // modes
    both = jnp.concatenate([early_ref[...], force_ref[...]], axis=0).astype(F32)
    total = both.shape[0]
    pair[0:16, :] = jnp.zeros((16, 2 * modes), F32)
    pair[16:, 0:modes] = both
    pair[0:17, modes:] = jnp.zeros((17, modes), F32)
    pair[17:16 + total, modes:] = both[:-1]
    for c in range(4):
        for i in range(2):
            d = 4 * c + 2 * i
            shifts[c, :, 128 * i:128 * i + 128] = pair[16 - d:16 - d + total, :].astype(BF16)
    first = steps - 3 * quarter
    rows = steps + 3 * quarter

    acc[...] = jnp.zeros_like(acc)

    def step(p, carry):
        top = pl.multiple_of(first - 16 * p, 16)
        left = jnp.concatenate([shifts[c, pl.ds(top, rows), :] for c in range(4)], axis=1)
        acc[...] += jnp.dot(left, weights[pl.ds(pl.multiple_of(p * 1024, 1024), 1024), :], preferred_element_type=F32)
        return carry

    lax.fori_loop(0, quarter // 16, step, 0)
    lane = lax.broadcasted_iota(I32, (steps, 2 * modes), 1) < modes
    def y(q, c):
        a = 3 * quarter - q * quarter
        return acc[a:a + steps, 128 * c:128 * c + 128]
    s = jnp.where(lane, y(0, 0), y(1, 0)) + jnp.where(lane, y(2, 1), y(3, 1))
    response = (s[:, :modes] + s[:, modes:]).astype(BF16)
    out_ref[...] = lax.dot_general(map_ref[...].reshape(-1, modes), response, (((1,), (1,)), ((), ())), preferred_element_type=F32).astype(BF16)


def local_stress(early, force, weights, whole_map):
    steps, modes = force.shape
    quarter = weights.shape[0] // modes
    owners, own = whole_map.shape[0], 8
    total = 2 * steps
    return pl.pallas_call(
        response_kernel,
        out_shape=jax.ShapeDtypeStruct((owners * own, steps), BF16),
        grid=(1,),
        in_specs=[pl.BlockSpec(memory_space=pltpu.VMEM)] * 3 + [whole((owners, own, modes))],
        out_specs=pl.BlockSpec(memory_space=pltpu.VMEM),
        scratch_shapes=[
            pltpu.VMEM((total + 16, 2 * modes), F32),
            pltpu.VMEM((4, total, 4 * modes), BF16),
            pltpu.VMEM((steps + 3 * quarter, 256), F32),
        ],
        compiler_params=pltpu.CompilerParams(vmem_limit_bytes=12 * 1024 * 1024),
        cost_estimate=pl.CostEstimate(flops=4 * 10 ** 9, bytes_accessed=4 * 10 ** 6, transcendentals=0),
        name="local_stress",
    )(early, force, weights, whole_map)


def shifted(value, axis, steps):
    count = lax.axis_size(axis)
    leading, last = (max(0, -steps), min(count, count - steps))
    return lax.ppermute(value, axis, [(source, source + steps) for source in range(leading, last)])


def body(wet_station, wet_girth, wet_count, pressure, panel_area, panel_patch, patch_modes, impulse, stress_map):
    steps = wet_station.shape[0]
    lags = impulse.shape[0]
    own_map = lax.optimization_barrier(jnp.tile(stress_map.T[None], (lax.axis_size("tm"), 1, 1)))
    whole_map = lax.all_to_all(own_map, "tm", 0, 0, tiled=True)
    weights = impulse_weights(impulse)
    force = forcing(wet_station, wet_girth, wet_count, pressure, panel_area, panel_patch, patch_modes)
    early = shifted(force, "tm", 1)
    part = local_stress(early, force, weights, whole_map)
    return lax.all_to_all(part, "tm", 0, 1, tiled=True)


def solution(mesh):
    return jax.shard_map(
        body,
        mesh=mesh,
        in_specs=(
            P(("sea", "tm"), None),
            P(("sea", "tm"), None),
            P(("sea", "tm")),
            P(("sea", "tm"), None),
            P(),
            P(),
            P(),
            P(),
            P(None, "tm"),
        ),
        out_specs=P("tm", "sea"),
        check_vma=False,
    )
```

```python
import functools

import jax
import jax.numpy as jnp
from jax import lax
from jax.experimental import pallas as pl
from jax.experimental.pallas import tpu as pltpu
from jax.sharding import PartitionSpec as P

F32, BF16, I32 = jnp.float32, jnp.bfloat16, jnp.int32
GIRTH = 500
LANES = 128
HALF = 200
AREA_SCALE = 32767.0


def pow2_up(x, e, bits):
    for b in range(bits):
        x = jnp.where((e & (1 << b)) != 0, x * float(2 ** (1 << b)), x)
    return x


def pow2_down(x, bits, top):
    e = jnp.zeros(x.shape, I32)
    for b in reversed(range(bits)):
        big = x >= float(top * 2 ** ((1 << b)))
        x = jnp.where(big, x * float(2.0 ** -(1 << b)), x)
        e = e + jnp.where(big, jnp.int32(1 << b), jnp.int32(0))
    return x, e


def shuffled(x, sub):
    x = list(x)
    for k in (1, 2, 4):
        keep = (sub & k) == 0
        for i in range(8):
            if i & k == 0:
                u, v = x[i], x[i | k]
                x[i] = jnp.where(keep, u, pltpu.roll(v, k, 0))
                x[i | k] = jnp.where(keep, pltpu.roll(u, 8 - k, 0), v)
    return x


def forcing_kernel(st_any, gi_any, cnt_any, pr_any, modes_any, first_ref, second_ref, out_ref,
                   st_ref, gi_ref, cnt_ref, pr_ref, modes_ref, sems, tab, xs, sc, sr, sp,
                   pc, prow, pp, sel1, sel2, fhv, flv, hiv, lov, wt, rankc):
    steps = st_ref.shape[0]
    modes = modes_ref.shape[0]
    blocks = steps // LANES
    copies = [pltpu.make_async_copy(x, y, sems.at[i]) for i, (x, y) in enumerate((
        (cnt_any, cnt_ref), (st_any, st_ref), (gi_any, gi_ref), (pr_any, pr_ref), (modes_any, modes_ref)))]
    for c in copies:
        c.start()
    for h in range(2):
        for part, ref in enumerate((first_ref, second_ref)):
            tab[HALF * part:HALF * (part + 1), LANES * h:LANES * (h + 1)] = ref[HALF * h:HALF * (h + 1), :]
    sub = lax.broadcasted_iota(I32, (8, LANES), 0)
    slot = lax.broadcasted_iota(I32, (LANES, LANES), 1).astype(F32)
    line = lax.broadcasted_iota(I32, (LANES, LANES), 0).astype(F32)
    copies[0].wait()
    counts = cnt_ref[...].astype(F32)
    n64 = jnp.sum(jnp.where(counts > 64.0, 1.0, 0.0)).astype(I32)
    n32 = jnp.sum(jnp.where(counts > 32.0, 1.0, 0.0)).astype(I32)
    lane_row = lax.broadcasted_iota(I32, (1, LANES), 1).astype(F32)
    count_row = [counts[j:j + 1, :] for j in range(blocks)]
    key_row = [count_row[j] * float(steps) + (float(steps - 1 - LANES * j) - lane_row) for j in range(blocks)]
    count_col = [jnp.broadcast_to(count_row[j], (LANES, LANES)).T for j in range(blocks)]
    key_col = [count_col[j] * float(steps) + (float(steps - 1 - LANES * j) - line) for j in range(blocks)]
    rank_row = []
    for j in range(blocks):
        above = jnp.zeros((8, LANES), F32)
        for i in range(blocks):
            for v in range(LANES // 8):
                above = above + jnp.where(key_col[i][8 * v:8 * v + 8] > key_row[j], 1.0, 0.0)
        rank_row.append(jnp.sum(above, axis=0, keepdims=True))
        rankc[LANES * j:LANES * (j + 1), :] = jnp.broadcast_to(rank_row[j], (LANES, LANES)).T
    for c in copies[1:4]:
        c.wait()
    for j in range(blocks):
        here = slice(LANES * j, LANES * (j + 1))
        panel = st_ref[here, :] * GIRTH + gi_ref[here, :]
        hi = panel >> 7
        second = hi >= HALF
        xs[here, 0:LANES] = ((panel & 127) + jnp.where(second, LANES, 0)).astype(F32).astype(BF16)
        xs[here, LANES:2 * LANES] = jnp.where(second, hi - HALF, hi).astype(F32).astype(BF16)
        xs[here, 2 * LANES:] = jnp.where(slot < count_col[j], pr_ref[here, :].astype(F32), 0.0).astype(BF16)
    for j in range(blocks):
        here = slice(LANES * j, LANES * (j + 1))
        place = jnp.concatenate([jnp.where(rank_row[i] == line + float(LANES * j), 1.0, 0.0).astype(BF16) for i in range(blocks)], axis=1)
        y = jnp.dot(place, xs[...], preferred_element_type=F32)
        for i, ref in enumerate((sc, sr, sp)):
            ref[here, :] = y[:, LANES * i:LANES * (i + 1)]
    for ref in (sc, sr, sp):
        ref[steps:, :] = jnp.zeros((LANES, LANES), F32)

    group = LANES // 4
    n_full = (n64 + (group - 1)) // group
    base2 = n_full * group
    n_half = (jnp.maximum(n32 - base2, 0) + (2 * group - 1)) // (2 * group)
    base4 = base2 + n_half * 2 * group
    n_quarter = (jnp.maximum(steps - base4, 0) + (4 * group - 1)) // (4 * group)
    n_all = n_full + n_half + n_quarter
    firsts = {1: (n_full, 0, 0), 2: (n_half, base2, n_full), 4: (n_quarter, base4, n_full + n_half)}
    lane = lax.broadcasted_iota(I32, (group, LANES), 1)

    for pack, (n, start, where) in firsts.items():
        def gather(g, carry, pack=pack, start=start, where=where):
            source = start + g * (group * pack)
            target = pl.multiple_of((where + g) * group, group)
            for s_ref, p_ref in ((sc, pc), (sr, prow), (sp, pp)):
                x = s_ref[pl.ds(pl.multiple_of(source, group), group), :]
                for c in range(1, pack):
                    y = s_ref[pl.ds(pl.multiple_of(source + group * c, group), group), :]
                    x = jnp.where(lane < LANES // pack * c, x, pltpu.roll(y, LANES // pack * c, 1))
                p_ref[pl.ds(target, group), :] = x
            return carry
        lax.fori_loop(0, n, gather, 0)

    iota_b = lax.broadcasted_iota(I32, (256, LANES), 0).astype(F32).astype(BF16)
    one = jnp.ones((), BF16)
    zero = jnp.zeros((), BF16)

    def onehot(row_f32, depth):
        b = jnp.broadcast_to(row_f32, (depth, LANES)).astype(BF16)
        return jnp.where(iota_b[:depth] == b, one, zero)

    def stage1_pair(t0):
        oh = jnp.concatenate([onehot(pc[pl.ds(t0 + j, 1), :], 256) for j in range(2)], axis=1)
        r = jnp.dot(tab[...], oh, preferred_element_type=F32)
        for j in range(2):
            want = jnp.broadcast_to(prow[pl.ds(t0 + j, 1), :].astype(I32), (8, LANES)) - sub
            a1 = jnp.zeros((8, LANES), F32)
            a2 = jnp.zeros((8, LANES), F32)
            for v in range(HALF // 8):
                hit = want == 8 * v
                a1 = jnp.where(hit, r[8 * v:8 * v + 8, LANES * j:LANES * (j + 1)], a1)
                a2 = jnp.where(hit, r[HALF + 8 * v:HALF + 8 * v + 8, LANES * j:LANES * (j + 1)], a2)
            sel1[pl.ds(t0 + j, 1), :] = jnp.sum(a1, axis=0, keepdims=True)
            sel2[pl.ds(t0 + j, 1), :] = jnp.sum(a2, axis=0, keepdims=True)

    def decode(base, count):
        here = pl.ds(base, count)
        x1 = sel1[here, :]
        x2 = sel2[here, :]
        m1, e1 = pow2_down(jnp.abs(x1), 6, 128)
        m2, e2 = pow2_down(jnp.abs(x2), 6, 128)
        qi = (m1.astype(I32) - 128) + (e1 << 7) + jnp.where(x1 < 0, 1 << 13, 0) + jnp.where(x2 < 0, 1 << 14, 0) + ((e2 & 1) << 15)
        f = pp[here, :] * (qi.astype(F32) * (1.0 / AREA_SCALE))
        high = f.astype(BF16).astype(F32)
        fhv[here, :] = high
        flv[here, :] = f - high
        lov[here, :] = m2 - 128.0
        hiv[here, :] = e2 >> 1

    sel1[0:group, :] = jnp.full((group, LANES), 128.0, F32)
    sel2[0:group, :] = jnp.full((group, LANES), 128.0, F32)

    def lookup(g, carry):
        before = pl.multiple_of(jnp.maximum(g - 1, 0) * group, group)
        base = pl.multiple_of(g * group, group)
        for p in range(group // 2):
            stage1_pair(base + 2 * p)
            if p % 4 == 1:
                decode(pl.multiple_of(before + 8 * (p // 4), 8), 8)
        return carry

    lax.fori_loop(0, n_all, lookup, 0)
    decode(pl.multiple_of((n_all - 1) * group, group), group)


    high_parts = wt.shape[0]
    iota_h = lax.broadcasted_iota(I32, (high_parts, LANES), 0)
    chunk_lane = lax.broadcasted_iota(I32, (2 * high_parts, LANES), 1)

    for pack, (n, start, where) in firsts.items():
        def scatter(g, carry, pack=pack, start=start, where=where):
            packed = (where + g) * group
            place = start + g * (group * pack)
            for o in range(group // 8):
                sums = [[None] * 8 for _ in range(pack)]
                for p in range(4):
                    rows = []
                    hots = []
                    for j in range(2):
                        t = pl.ds(packed + 8 * o + 2 * p + j, 1)
                        hots.append(onehot(lov[t, :], LANES))
                        hit = jnp.broadcast_to(hiv[t, :], (high_parts, LANES)) == iota_h
                        high = jnp.where(hit, jnp.broadcast_to(fhv[t, :], (high_parts, LANES)), 0.0)
                        low = jnp.where(hit, jnp.broadcast_to(flv[t, :], (high_parts, LANES)), 0.0)
                        both = jnp.concatenate([high, low], axis=0)
                        for c in range(pack):
                            if pack > 1:
                                width = LANES // pack
                                mine = jnp.where((chunk_lane >= width * c) & (chunk_lane < width * (c + 1)), both, 0.0)
                            else:
                                mine = both
                            mine = mine.astype(BF16)
                            none = jnp.zeros_like(mine)
                            rows.append(jnp.concatenate([mine, none] if j == 0 else [none, mine], axis=1))
                    w = lax.dot_general(jnp.concatenate(rows, axis=0), jnp.concatenate(hots, axis=1),
                                        (((1,), (1,)), ((), ())), preferred_element_type=F32)
                    for j in range(2):
                        for c in range(pack):
                            at = 2 * high_parts * (j * pack + c)
                            sums[c][2 * p + j] = w[at:at + high_parts] + w[at + high_parts:at + 2 * high_parts]
                for c in range(pack):
                    spot = pl.ds(pl.multiple_of(place + group * c + 8 * o, 8), 8)
                    for hb in range(high_parts // 8):
                        for i, x in enumerate(shuffled([y[8 * hb:8 * hb + 8] for y in sums[c]], sub)):
                            wt[8 * hb + i, spot, :] = x
            return carry
        lax.fori_loop(0, n, scatter, 0)

    copies[4].wait()
    ordered = []
    for j in range(blocks):
        here = slice(LANES * j, LANES * (j + 1))
        acc = jnp.zeros((2 * LANES, modes), F32)
        for h in range(high_parts // 2):
            w = jnp.concatenate([wt[2 * h, here, :], wt[2 * h + 1, here, :]], axis=1)
            wh = w.astype(BF16)
            wl = (w - wh.astype(F32)).astype(BF16)
            acc = acc + lax.dot_general(jnp.concatenate([wh, wl], axis=0), modes_ref[:, 256 * h:256 * h + 256],
                                        (((1,), (1,)), ((), ())), preferred_element_type=F32)
        ordered.append((acc[:LANES] + acc[LANES:]).astype(BF16))
    ordered = jnp.concatenate(ordered, axis=0)
    for j in range(blocks):
        here = slice(LANES * j, LANES * (j + 1))
        back = jnp.concatenate([jnp.where(rankc[here, :] == slot + float(LANES * i), 1.0, 0.0).astype(BF16) for i in range(blocks)], axis=1)
        out_ref[here, :] = jnp.dot(back, ordered, preferred_element_type=F32).astype(BF16)


def whole(shape):
    return pl.BlockSpec(shape, lambda i: (0,) * len(shape))


def encoded(panel_area, panel_patch):
    pad = 2 * HALF * LANES - panel_area.shape[0]
    q = (jnp.pad(panel_area, (0, pad)) * AREA_SCALE + 0.5).astype(I32)
    patch = jnp.pad(panel_patch, (0, pad))
    first = pow2_up(((q & 127) + 128).astype(F32), (q >> 7) & 63, 6)
    first = jnp.where(((q >> 13) & 1) == 1, -first, first).astype(BF16)
    second = pow2_up(((patch & 127) + 128).astype(F32), (patch >> 7) * 2 + (q >> 15), 6)
    second = jnp.where(((q >> 14) & 1) == 1, -second, second).astype(BF16)
    return first.reshape(2 * HALF, LANES), second.reshape(2 * HALF, LANES)


def forcing(wet_station, wet_girth, wet_count, pressure, panel_area, panel_patch, patch_modes):
    steps = wet_station.shape[0]
    patches, modes = patch_modes.shape
    first, second = encoded(panel_area, panel_patch)
    far = (wet_station, wet_girth, wet_count.reshape(steps // LANES, LANES), pressure, patch_modes.T)
    far = tuple(pltpu.with_memory_space_constraint(x, pltpu.HBM) for x in far)
    table = lambda n, t: pltpu.VMEM((n, LANES), t)
    return pl.pallas_call(
        forcing_kernel,
        out_shape=jax.ShapeDtypeStruct((steps, modes), BF16),
        in_specs=[pl.BlockSpec(memory_space=pltpu.HBM)] * 5 + [pl.BlockSpec(memory_space=pltpu.VMEM)] * 2,
        out_specs=pl.BlockSpec(memory_space=pltpu.VMEM),
        scratch_shapes=[
            *[pltpu.VMEM(x.shape, x.dtype) for x in far],
            pltpu.SemaphoreType.DMA((5,)),
            pltpu.VMEM((2 * HALF, 256), BF16),
            pltpu.VMEM((steps, 3 * LANES), BF16),
            *[table(steps + LANES, F32)] * 3,
            *[table(steps, F32)] * 7,
            table(steps, I32), table(steps, F32),
            pltpu.VMEM((patches // LANES, steps + LANES, LANES), F32),
            table(steps, F32),
        ],
        compiler_params=pltpu.CompilerParams(vmem_limit_bytes=24 * 1024 * 1024),
        cost_estimate=pl.CostEstimate(flops=2 * 10 ** 10, bytes_accessed=2 * 10 ** 6, transcendentals=0),
        name="forcing",
    )(*far, first, second)


def weights_kernel(imp_ref, out_ref):
    modes = out_ref.shape[1] // 4
    quarter = imp_ref.shape[1] // 4
    row = lax.broadcasted_iota(I32, (2 * quarter, 2 * quarter), 0)
    col = lax.broadcasted_iota(I32, (2 * quarter, 2 * quarter), 1)
    order = jnp.where(((row >> 3) & 1) * quarter + (row >> 4) * 8 + (row & 7) == col, 1.0, 0.0).astype(BF16)

    def turn(i, carry):
        pair = [imp_ref[pl.ds(pl.multiple_of((2 * i + m) * modes, modes), modes), :] for m in range(2)]
        block = jnp.concatenate([jnp.concatenate([x[:, quarter * q:quarter * (q + 1)] for x in pair], axis=1) for q in range(4)], axis=0)
        y = lax.dot_general(order, block, (((1,), (1,)), ((), ())), preferred_element_type=F32).astype(BF16)
        for v in range(quarter // 8):
            out_ref[pl.ds(pl.multiple_of(v * (8 * modes) + 16 * i, 16), 16), :] = y[16 * v:16 * v + 16]
        return carry

    lax.fori_loop(0, modes // 2, turn, 0, unroll=8)


def impulse_weights(impulse):
    lags, modes, _ = impulse.shape
    flat = jnp.transpose(impulse, (1, 2, 0)).reshape(modes * modes, lags)
    return pl.pallas_call(
        weights_kernel,
        out_shape=jax.ShapeDtypeStruct((lags // 4 * modes, 4 * modes), BF16),
        in_specs=[pl.BlockSpec(memory_space=pltpu.VMEM)],
        out_specs=pl.BlockSpec(memory_space=pltpu.VMEM),
        compiler_params=pltpu.CompilerParams(vmem_limit_bytes=8 * 1024 * 1024),
        cost_estimate=pl.CostEstimate(flops=3 * 10 ** 9, bytes_accessed=8 * 10 ** 6, transcendentals=0),
        name="impulse_weights",
    )(flat)


def products(seq, wts, pair, x8, shifts, acc):
    count, modes = seq.shape
    depth = 16 * modes
    steps = wts.shape[0] // depth
    quarter = 16 * steps
    pair[0:8, :] = jnp.zeros((8, 2 * modes), F32)
    pair[8:, 0:modes] = seq
    pair[0:9, modes:] = jnp.zeros((9, modes), F32)
    pair[9:8 + count, modes:] = seq[:-1]
    for i in range(4):
        x8[:, 2 * modes * i:2 * modes * (i + 1)] = pair[8 - 2 * i:8 - 2 * i + count, :].astype(BF16)
    row = lax.broadcasted_iota(I32, (8 * modes, 8 * modes), 0)
    col = lax.broadcasted_iota(I32, (8 * modes, 8 * modes), 1)
    spread = jnp.where((row & (modes - 1)) * 8 + row // modes == col, 1.0, 0.0).astype(BF16)
    last = jnp.zeros((8, 8 * modes), F32)
    for k in range(count // LANES):
        here = slice(LANES * k, LANES * (k + 1))
        y = jnp.dot(x8[here, :], spread, preferred_element_type=F32)
        shifts[here, 0:8 * modes] = y.astype(BF16)
        shifts[here, 8 * modes:] = jnp.concatenate([last, y[:-8]], axis=0).astype(BF16)
        last = y[-8:]
    cut = depth // 2
    halves = [None, None]
    for p in range(steps):
        left = shifts[quarter - 16 * p:count - 16 * p, :]
        for i in range(2):
            part = jnp.dot(left[:, cut * i:cut * (i + 1)], wts[depth * p + cut * i:depth * p + cut * (i + 1), :], preferred_element_type=F32)
            halves[i] = part if p == 0 else halves[i] + part
    acc[...] = halves[0] + halves[1]


def stress_kernel(early_ref, force_ref, map_ref, wts, out_ref, pair, x8, shifts, acc):
    steps, modes = force_ref.shape
    quarter = wts.shape[0] // modes
    seq = jnp.concatenate([early_ref[...], force_ref[...]], axis=0).astype(F32)
    products(seq, wts, pair, x8, shifts, acc)

    def y(q):
        return acc[(3 - q) * quarter:(3 - q) * quarter + steps, 128 * (q // 2):128 * (q // 2) + 128]

    lane = lax.broadcasted_iota(I32, (steps, 2 * modes), 1) < modes
    s = jnp.where(lane, y(0), y(1)) + jnp.where(lane, y(2), y(3))
    response = (s[:, :modes] + s[:, modes:]).astype(BF16)
    flat = map_ref[...].reshape(-1, map_ref.shape[2])
    lines, folds = flat.shape[0], flat.shape[1] // modes
    parts = jnp.concatenate([flat[:, modes * b:modes * (b + 1)] for b in range(folds)], axis=0)
    row = lax.broadcasted_iota(I32, (lines * folds, lines * folds), 0)
    col = lax.broadcasted_iota(I32, (lines * folds, lines * folds), 1)
    order = jnp.where((row & (folds - 1)) * lines + row // folds == col, 1.0, 0.0).astype(BF16)
    hot_map = jnp.dot(order, parts, preferred_element_type=F32).astype(BF16)
    out_ref[...] = lax.dot_general(hot_map, response, (((1,), (1,)), ((), ())), preferred_element_type=F32).astype(BF16)


def work(count, modes):
    return [
        pltpu.VMEM((count + 8, 2 * modes), F32),
        pltpu.VMEM((count, 8 * modes), BF16),
        pltpu.VMEM((count, 16 * modes), BF16),
    ]


def local_stress(early, force, whole_map, weights):
    steps, modes = force.shape
    quarter = weights.shape[0] // modes
    hot = whole_map.size // modes
    return pl.pallas_call(
        stress_kernel,
        out_shape=jax.ShapeDtypeStruct((hot, steps), BF16),
        in_specs=[pl.BlockSpec(memory_space=pltpu.VMEM)] * 4,
        out_specs=pl.BlockSpec(memory_space=pltpu.VMEM),
        scratch_shapes=[*work(2 * steps, modes), pltpu.VMEM((2 * steps - quarter, 4 * modes), F32)],
        compiler_params=pltpu.CompilerParams(vmem_limit_bytes=20480 * 1024),
        cost_estimate=pl.CostEstimate(flops=4 * 10 ** 9, bytes_accessed=5 * 10 ** 6, transcendentals=0),
        name="local_stress",
    )(early, force, whole_map, weights)


def shifted(value, axis, steps):
    count = lax.axis_size(axis)
    leading, last = (max(0, -steps), min(count, count - steps))
    return lax.ppermute(value, axis, [(source, source + steps) for source in range(leading, last)])


def body(wet_station, wet_girth, wet_count, pressure, panel_area, panel_patch, patch_modes, impulse, stress_map):
    steps = wet_station.shape[0]
    own_map = jnp.tile(stress_map.T.reshape(1, -1, 256), (lax.axis_size("tm"), 1, 1))
    whole_map = lax.all_to_all(own_map, "tm", 0, 0, tiled=True)
    force = forcing(wet_station, wet_girth, wet_count, pressure, panel_area, panel_patch, patch_modes)
    force, whole_map = lax.optimization_barrier((force, whole_map))
    early = shifted(force, "tm", 1)
    weights = pltpu.with_memory_space_constraint(impulse_weights(impulse), pltpu.VMEM)
    part = local_stress(early, force, whole_map, weights)
    return lax.all_to_all(part, "tm", 0, 1, tiled=True)


def solution(mesh):
    return jax.shard_map(
        body,
        mesh=mesh,
        in_specs=(
            P(("sea", "tm"), None),
            P(("sea", "tm"), None),
            P(("sea", "tm")),
            P(("sea", "tm"), None),
            P(),
            P(),
            P(),
            P(),
            P(None, "tm"),
        ),
        out_specs=P("tm", "sea"),
        check_vma=False,
    )
```

```python
import functools

import jax
import jax.numpy as jnp
from jax import lax
from jax.experimental import pallas as pl
from jax.experimental.pallas import tpu as pltpu
from jax.sharding import PartitionSpec as P

F32, BF16, I32 = jnp.float32, jnp.bfloat16, jnp.int32
GIRTH = 500
LANES = 128
HALF = 200
CUT = 104
LEAST = 0.2
CODES = 1023.0
DECADE = 3.3219280948873626
BIAS = 2.0 ** -70


def pow2_up(x, e, bits):
    for b in range(bits):
        x = jnp.where((e & (1 << b)) != 0, x * float(2 ** (1 << b)), x)
    return x


def pow2_down(x, bits):
    e = jnp.zeros(x.shape, I32)
    for b in reversed(range(bits)):
        big = x >= 128.0 * BIAS * 2.0 ** (1 << b)
        x = jnp.where(big, x * float(2.0 ** -(1 << b)), x)
        e = e + jnp.where(big, jnp.int32(1 << b), jnp.int32(0))
    return x * (1.0 / BIAS), e


def shuffled(x, sub):
    x = list(x)
    for k in (1, 2, 4):
        keep = (sub & k) == 0
        for i in range(8):
            if i & k == 0:
                u, v = x[i], x[i | k]
                x[i] = jnp.where(keep, u, pltpu.roll(v, k, 0))
                x[i | k] = jnp.where(keep, pltpu.roll(u, 8 - k, 0), v)
    return x


def forcing_kernel(st_any, gi_any, cnt_any, pr_any, modes_any, word_ref, out_ref,
                   st_ref, gi_ref, cnt_ref, pr_ref, modes_ref, sems, tab, xs, sc, sr, sp,
                   pc, prow, pp, sel1, sel2, fhv, flv, hiv, lov, wt, rankc):
    steps = st_ref.shape[0]
    modes = modes_ref.shape[0]
    blocks = steps // LANES
    copies = [pltpu.make_async_copy(x, y, sems.at[i]) for i, (x, y) in enumerate((
        (cnt_any, cnt_ref), (st_any, st_ref), (gi_any, gi_ref), (pr_any, pr_ref), (modes_any, modes_ref)))]
    for c in copies:
        c.start()
    for h in range(2):
        lanes = slice(LANES * h, LANES * (h + 1))
        word = word_ref[HALF * h:HALF * (h + 1), :]
        first = pow2_up(((word & 127) + 128).astype(F32) * BIAS, ((word >> 7) & 31) + ((word >> 12) & 3) * 32, 7)
        tab[0:HALF, lanes] = jnp.where((word & (4 << 12)) != 0, -first, first).astype(BF16)
        upper = word >> 15
        other = jnp.concatenate([upper[CUT:], jnp.zeros((2 * CUT - HALF, LANES), I32)], axis=0)
        tab[HALF:, lanes] = pow2_up((upper[:CUT] + 128).astype(F32) * BIAS, other, 7).astype(BF16)
    sub = lax.broadcasted_iota(I32, (8, LANES), 0)
    slot = lax.broadcasted_iota(I32, (LANES, LANES), 1).astype(F32)
    line = lax.broadcasted_iota(I32, (LANES, LANES), 0).astype(F32)
    line2 = lax.broadcasted_iota(I32, (2 * LANES, LANES), 0).astype(F32)
    copies[0].wait()
    counts = cnt_ref[...].astype(F32)
    n64 = jnp.sum(jnp.where(counts > 64.0, 1.0, 0.0)).astype(I32)
    n32 = jnp.sum(jnp.where(counts > 32.0, 1.0, 0.0)).astype(I32)
    lane_row = lax.broadcasted_iota(I32, (1, LANES), 1).astype(F32)
    count_row = [counts[j:j + 1, :] for j in range(blocks)]
    key_row = [count_row[j] * float(steps) + (float(steps - 1 - LANES * j) - lane_row) for j in range(blocks)]
    count_col = [jnp.broadcast_to(count_row[j], (LANES, LANES)).T for j in range(blocks)]
    key_col = [count_col[j] * float(steps) + (float(steps - 1 - LANES * j) - line) for j in range(blocks)]
    rank_row = []
    for j in range(blocks):
        above = jnp.zeros((8, LANES), F32)
        for i in range(blocks):
            for v in range(LANES // 8):
                above = above + jnp.where(key_col[i][8 * v:8 * v + 8] > key_row[j], 1.0, 0.0)
        rank_row.append(jnp.sum(above, axis=0, keepdims=True))
        rankc[LANES * j:LANES * (j + 1), :] = jnp.broadcast_to(rank_row[j], (LANES, LANES)).T
    for c in copies[1:4]:
        c.wait()
    for j in range(blocks):
        here = slice(LANES * j, LANES * (j + 1))
        panel = st_ref[here, :] * GIRTH + gi_ref[here, :]
        hi = panel >> 7
        second = hi >= HALF
        xs[here, 0:LANES] = ((panel & 127) + jnp.where(second, LANES, 0)).astype(F32).astype(BF16)
        xs[here, LANES:2 * LANES] = jnp.where(second, hi - HALF, hi).astype(F32).astype(BF16)
        xs[here, 2 * LANES:] = jnp.where(slot < count_col[j], pr_ref[here, :].astype(F32), 0.0).astype(BF16)
    for j in range(blocks // 2):
        here = slice(2 * LANES * j, 2 * LANES * (j + 1))
        place = jnp.concatenate([jnp.where(rank_row[i] == line2 + float(2 * LANES * j), 1.0, 0.0).astype(BF16) for i in range(blocks)], axis=1)
        y = jnp.dot(place, xs[...], preferred_element_type=F32)
        for i, ref in enumerate((sc, sr, sp)):
            ref[here, :] = y[:, LANES * i:LANES * (i + 1)]
    for ref in (sc, sr, sp):
        ref[steps:, :] = jnp.zeros((LANES, LANES), F32)

    group = LANES // 4
    n_full = (n64 + (group - 1)) // group
    base2 = n_full * group
    n_half = (jnp.maximum(n32 - base2, 0) + (2 * group - 1)) // (2 * group)
    base4 = base2 + n_half * 2 * group
    n_quarter = (jnp.maximum(steps - base4, 0) + (4 * group - 1)) // (4 * group)
    n_all = n_full + n_half + n_quarter
    firsts = {1: (n_full, 0, 0), 2: (n_half, base2, n_full), 4: (n_quarter, base4, n_full + n_half)}
    lane = lax.broadcasted_iota(I32, (group, LANES), 1)

    for pack, (n, start, where) in firsts.items():
        def gather(g, carry, pack=pack, start=start, where=where):
            source = start + g * (group * pack)
            target = pl.multiple_of((where + g) * group, group)
            for s_ref, p_ref in ((sc, pc), (sr, prow), (sp, pp)):
                x = s_ref[pl.ds(pl.multiple_of(source, group), group), :]
                for c in range(1, pack):
                    y = s_ref[pl.ds(pl.multiple_of(source + group * c, group), group), :]
                    x = jnp.where(lane < LANES // pack * c, x, pltpu.roll(y, LANES // pack * c, 1))
                p_ref[pl.ds(target, group), :] = x
            return carry
        lax.fori_loop(0, n, gather, 0)

    iota_b = lax.broadcasted_iota(I32, (256, LANES), 0).astype(F32).astype(BF16)
    one = jnp.ones((), BF16)
    zero = jnp.zeros((), BF16)

    def onehot(row_f32, depth):
        b = jnp.broadcast_to(row_f32, (depth, LANES)).astype(BF16)
        return jnp.where(iota_b[:depth] == b, one, zero)

    def stage1_pair(t0):
        oh = jnp.concatenate([onehot(pc[pl.ds(t0 + j, 1), :], 256) for j in range(2)], axis=1)
        r = jnp.dot(tab[...], oh, preferred_element_type=F32)
        for j in range(2):
            want = jnp.broadcast_to(prow[pl.ds(t0 + j, 1), :].astype(I32), (8, LANES)) - sub
            a1 = jnp.zeros((8, LANES), F32)
            a2 = jnp.zeros((8, LANES), F32)
            for v in range(HALF // 8):
                hit = want == 8 * v
                a1 = jnp.where(hit, r[8 * v:8 * v + 8, LANES * j:LANES * (j + 1)], a1)
                if 8 * v < CUT:
                    shared = hit | (want == 8 * v + CUT)
                    a2 = jnp.where(shared, r[HALF + 8 * v:HALF + 8 * v + 8, LANES * j:LANES * (j + 1)], a2)
            sel1[pl.ds(t0 + j, 1), :] = jnp.sum(a1, axis=0, keepdims=True)
            sel2[pl.ds(t0 + j, 1), :] = jnp.sum(a2, axis=0, keepdims=True)

    def decode(base, count):
        here = pl.ds(base, count)
        x1 = sel1[here, :]
        x2 = sel2[here, :]
        m1, e1 = pow2_down(jnp.abs(x1), 7)
        m2, e2 = pow2_down(x2, 7)
        upper = jnp.where(prow[here, :] >= float(CUT), e2, m2.astype(I32) - 128)
        code = (upper << 3) + jnp.where(x1 < 0, 4, 0) + (e1 >> 5)
        f = pp[here, :] * (LEAST * jnp.exp2(code.astype(F32) * (DECADE / CODES)))
        high = f.astype(BF16).astype(F32)
        fhv[here, :] = high
        flv[here, :] = f - high
        lov[here, :] = m1 - 128.0
        hiv[here, :] = e1 & 31

    sel1[0:group, :] = jnp.full((group, LANES), 128.0 * BIAS, F32)
    sel2[0:group, :] = jnp.full((group, LANES), 128.0 * BIAS, F32)

    def lookup(g, carry):
        before = pl.multiple_of(jnp.maximum(g - 1, 0) * group, group)
        base = pl.multiple_of(g * group, group)
        for p in range(group // 2):
            stage1_pair(base + 2 * p)
            if p % 4 == 1:
                decode(pl.multiple_of(before + 8 * (p // 4), 8), 8)
        return carry

    lax.fori_loop(0, n_all, lookup, 0)
    decode(pl.multiple_of((n_all - 1) * group, group), group)


    high_parts = wt.shape[0]
    iota_h = lax.broadcasted_iota(I32, (high_parts, LANES), 0)
    chunk_lane = lax.broadcasted_iota(I32, (2 * high_parts, LANES), 1)

    for pack, (n, start, where) in firsts.items():
        def scatter(g, carry, pack=pack, start=start, where=where):
            packed = (where + g) * group
            place = start + g * (group * pack)
            for o in range(group // 8):
                sums = [[None] * 8 for _ in range(pack)]
                for p in range(4):
                    rows = []
                    hots = []
                    for j in range(2):
                        t = pl.ds(packed + 8 * o + 2 * p + j, 1)
                        hots.append(onehot(lov[t, :], LANES))
                        hit = jnp.broadcast_to(hiv[t, :], (high_parts, LANES)) == iota_h
                        high = jnp.where(hit, jnp.broadcast_to(fhv[t, :], (high_parts, LANES)), 0.0)
                        low = jnp.where(hit, jnp.broadcast_to(flv[t, :], (high_parts, LANES)), 0.0)
                        both = jnp.concatenate([high, low], axis=0)
                        for c in range(pack):
                            if pack > 1:
                                width = LANES // pack
                                mine = jnp.where((chunk_lane >= width * c) & (chunk_lane < width * (c + 1)), both, 0.0)
                            else:
                                mine = both
                            mine = mine.astype(BF16)
                            none = jnp.zeros_like(mine)
                            rows.append(jnp.concatenate([mine, none] if j == 0 else [none, mine], axis=1))
                    w = lax.dot_general(jnp.concatenate(rows, axis=0), jnp.concatenate(hots, axis=1),
                                        (((1,), (1,)), ((), ())), preferred_element_type=F32)
                    for j in range(2):
                        for c in range(pack):
                            at = 2 * high_parts * (j * pack + c)
                            sums[c][2 * p + j] = w[at:at + high_parts] + w[at + high_parts:at + 2 * high_parts]
                for c in range(pack):
                    spot = pl.ds(pl.multiple_of(place + group * c + 8 * o, 8), 8)
                    for hb in range(high_parts // 8):
                        for i, x in enumerate(shuffled([y[8 * hb:8 * hb + 8] for y in sums[c]], sub)):
                            wt[8 * hb + i, spot, :] = x
            return carry
        lax.fori_loop(0, n, scatter, 0)

    copies[4].wait()
    ordered = []
    many = 2 * LANES
    for j in range(steps // many):
        here = slice(many * j, many * (j + 1))
        acc = jnp.zeros((2 * many, modes), F32)
        for h in range(high_parts // 2):
            w = jnp.concatenate([wt[2 * h, here, :], wt[2 * h + 1, here, :]], axis=1)
            wh = w.astype(BF16)
            wl = (w - wh.astype(F32)).astype(BF16)
            acc = acc + lax.dot_general(jnp.concatenate([wh, wl], axis=0), modes_ref[:, 256 * h:256 * h + 256],
                                        (((1,), (1,)), ((), ())), preferred_element_type=F32)
        ordered.append((acc[:many] + acc[many:]).astype(BF16))
    ordered = jnp.concatenate(ordered, axis=0)
    for j in range(blocks):
        here = slice(LANES * j, LANES * (j + 1))
        back = jnp.concatenate([jnp.where(rankc[here, :] == slot + float(LANES * i), 1.0, 0.0).astype(BF16) for i in range(blocks)], axis=1)
        out_ref[here, :] = jnp.dot(back, ordered, preferred_element_type=F32).astype(BF16)


def whole(shape):
    return pl.BlockSpec(shape, lambda i: (0,) * len(shape))


def encoded(panel_area, panel_patch):
    pad = 2 * HALF * LANES - panel_area.shape[0]
    code = jnp.clip((jnp.log2(panel_area * (1.0 / LEAST)) * (CODES / DECADE) + 0.5).astype(I32), 0, int(CODES))
    return jnp.pad(panel_patch + (code << 12), (0, pad)).reshape(2 * HALF, LANES)


def forcing(wet_station, wet_girth, wet_count, pressure, panel_area, panel_patch, patch_modes):
    steps = wet_station.shape[0]
    patches, modes = patch_modes.shape
    words = encoded(panel_area, panel_patch)
    far = (wet_station, wet_girth, wet_count.reshape(steps // LANES, LANES), pressure, patch_modes.T)
    far = tuple(pltpu.with_memory_space_constraint(x, pltpu.HBM) for x in far)
    table = lambda n, t: pltpu.VMEM((n, LANES), t)
    return pl.pallas_call(
        forcing_kernel,
        out_shape=jax.ShapeDtypeStruct((steps, modes), BF16),
        in_specs=[pl.BlockSpec(memory_space=pltpu.HBM)] * 5 + [pl.BlockSpec(memory_space=pltpu.VMEM)],
        out_specs=pl.BlockSpec(memory_space=pltpu.VMEM),
        scratch_shapes=[
            *[pltpu.VMEM(x.shape, x.dtype) for x in far],
            pltpu.SemaphoreType.DMA((5,)),
            pltpu.VMEM((HALF + CUT, 256), BF16),
            pltpu.VMEM((steps, 3 * LANES), BF16),
            *[table(steps + LANES, F32)] * 3,
            *[table(steps, F32)] * 7,
            table(steps, I32), table(steps, F32),
            pltpu.VMEM((patches // LANES, steps + LANES, LANES), F32),
            table(steps, F32),
        ],
        compiler_params=pltpu.CompilerParams(vmem_limit_bytes=24 * 1024 * 1024),
        cost_estimate=pl.CostEstimate(flops=2 * 10 ** 10, bytes_accessed=2 * 10 ** 6, transcendentals=0),
        name="forcing",
    )(*far, words)


def weights_kernel(imp_any, out_ref, imp_ref, sems):
    modes = out_ref.shape[1] // 4
    quarter = imp_ref.shape[1] // 4
    row = lax.broadcasted_iota(I32, (2 * quarter, 2 * quarter), 0)
    col = lax.broadcasted_iota(I32, (2 * quarter, 2 * quarter), 1)
    chunk = imp_ref.shape[0] // 4
    copies = [pltpu.make_async_copy(imp_any.at[pl.ds(chunk * c, chunk), :], imp_ref.at[pl.ds(chunk * c, chunk), :], sems.at[c]) for c in range(4)]
    for c in copies:
        c.start()
    order = jnp.where(((row >> 3) & 1) * quarter + (row >> 4) * 8 + (row & 7) == col, 1.0, 0.0).astype(BF16)

    def turn(i, carry):
        pair = [imp_ref[pl.ds(pl.multiple_of((2 * i + m) * modes, modes), modes), :] for m in range(2)]
        block = jnp.concatenate([jnp.concatenate([x[:, quarter * q:quarter * (q + 1)] for x in pair], axis=1) for q in range(4)], axis=0)
        y = lax.dot_general(order, block, (((1,), (1,)), ((), ())), preferred_element_type=F32).astype(BF16)
        for v in range(quarter // 8):
            out_ref[pl.ds(pl.multiple_of(v * (8 * modes) + 16 * i, 16), 16), :] = y[16 * v:16 * v + 16]
        return carry

    for c in range(4):
        copies[c].wait()
        lax.fori_loop(modes // 8 * c, modes // 8 * (c + 1), turn, 0, unroll=True)


def impulse_weights(impulse):
    lags, modes, _ = impulse.shape
    flat = jnp.transpose(impulse, (1, 2, 0)).reshape(modes * modes, lags)
    return pl.pallas_call(
        weights_kernel,
        out_shape=jax.ShapeDtypeStruct((lags // 4 * modes, 4 * modes), BF16),
        in_specs=[pl.BlockSpec(memory_space=pltpu.HBM)],
        out_specs=pl.BlockSpec(memory_space=pltpu.VMEM),
        scratch_shapes=[pltpu.VMEM(flat.shape, BF16), pltpu.SemaphoreType.DMA((4,))],
        compiler_params=pltpu.CompilerParams(vmem_limit_bytes=12 * 1024 * 1024),
        cost_estimate=pl.CostEstimate(flops=3 * 10 ** 9, bytes_accessed=8 * 10 ** 6, transcendentals=0),
        name="impulse_weights",
    )(pltpu.with_memory_space_constraint(flat, pltpu.HBM))


def products(seq, wts, pair, x8, shifts, acc):
    count, modes = seq.shape
    depth = 16 * modes
    steps = wts.shape[0] // depth
    quarter = 16 * steps
    pair[0:8, :] = jnp.zeros((8, 2 * modes), F32)
    pair[8:, 0:modes] = seq
    pair[0:9, modes:] = jnp.zeros((9, modes), F32)
    pair[9:8 + count, modes:] = seq[:-1]
    for i in range(4):
        x8[:, 2 * modes * i:2 * modes * (i + 1)] = pair[8 - 2 * i:8 - 2 * i + count, :].astype(BF16)
    row = lax.broadcasted_iota(I32, (8 * modes, 8 * modes), 0)
    col = lax.broadcasted_iota(I32, (8 * modes, 8 * modes), 1)
    spread = jnp.where((row & (modes - 1)) * 8 + row // modes == col, 1.0, 0.0).astype(BF16)
    last = jnp.zeros((8, 8 * modes), F32)
    big = 4 * LANES
    for k in range(count // big):
        here = slice(big * k, big * (k + 1))
        y = jnp.dot(x8[here, :], spread, preferred_element_type=F32)
        shifts[here, 0:8 * modes] = y.astype(BF16)
        shifts[here, 8 * modes:] = jnp.concatenate([last, y[:-8]], axis=0).astype(BF16)
        last = y[-8:]
    cut = depth // 2
    halves = [None, None]
    for p in range(steps):
        left = shifts[quarter - 16 * p:count - 16 * p, :]
        for i in range(2):
            part = jnp.dot(left[:, cut * i:cut * (i + 1)], wts[depth * p + cut * i:depth * p + cut * (i + 1), :], preferred_element_type=F32)
            halves[i] = part if p == 0 else halves[i] + part
    acc[...] = halves[0] + halves[1]


def stress_kernel(early_ref, force_ref, map_ref, wts, out_ref, pair, x8, shifts, acc):
    steps, modes = force_ref.shape
    quarter = wts.shape[0] // modes
    seq = jnp.concatenate([early_ref[...], force_ref[...]], axis=0).astype(F32)
    products(seq, wts, pair, x8, shifts, acc)

    def y(q):
        return acc[(3 - q) * quarter:(3 - q) * quarter + steps, 128 * (q // 2):128 * (q // 2) + 128]

    lane = lax.broadcasted_iota(I32, (steps, 2 * modes), 1) < modes
    s = jnp.where(lane, y(0), y(1)) + jnp.where(lane, y(2), y(3))
    response = (s[:, :modes] + s[:, modes:]).astype(BF16)
    hot_map = map_ref[...].reshape(-1, 2 * modes)[:, :modes]
    out_ref[...] = lax.dot_general(hot_map, response, (((1,), (1,)), ((), ())), preferred_element_type=F32).astype(BF16)


def work(count, modes):
    return [
        pltpu.VMEM((count + 8, 2 * modes), F32),
        pltpu.VMEM((count, 8 * modes), BF16),
        pltpu.VMEM((count, 16 * modes), BF16),
    ]


def local_stress(early, force, whole_map, weights):
    steps, modes = force.shape
    quarter = weights.shape[0] // modes
    hot = whole_map.shape[0] * whole_map.shape[1]
    return pl.pallas_call(
        stress_kernel,
        out_shape=jax.ShapeDtypeStruct((hot, steps), BF16),
        in_specs=[pl.BlockSpec(memory_space=pltpu.VMEM)] * 4,
        out_specs=pl.BlockSpec(memory_space=pltpu.VMEM),
        scratch_shapes=[*work(2 * steps, modes), pltpu.VMEM((2 * steps - quarter, 4 * modes), F32)],
        compiler_params=pltpu.CompilerParams(vmem_limit_bytes=20480 * 1024),
        cost_estimate=pl.CostEstimate(flops=4 * 10 ** 9, bytes_accessed=5 * 10 ** 6, transcendentals=0),
        name="local_stress",
    )(early, force, whole_map, weights)


def shifted(value, axis, steps):
    count = lax.axis_size(axis)
    leading, last = (max(0, -steps), min(count, count - steps))
    return lax.ppermute(value, axis, [(source, source + steps) for source in range(leading, last)])


def body(wet_station, wet_girth, wet_count, pressure, panel_area, panel_patch, patch_modes, impulse, stress_map):
    steps = wet_station.shape[0]
    own_map = jnp.tile(stress_map.T[None], (lax.axis_size("tm"), 1, 2))
    whole_map = lax.all_to_all(own_map, "tm", 0, 0, tiled=True)
    force = forcing(wet_station, wet_girth, wet_count, pressure, panel_area, panel_patch, patch_modes)
    force, whole_map = lax.optimization_barrier((force, whole_map))
    early = shifted(force, "tm", 1)
    weights = pltpu.with_memory_space_constraint(impulse_weights(impulse), pltpu.VMEM)
    part = local_stress(early, force, whole_map, weights)
    return lax.all_to_all(part, "tm", 0, 1, tiled=True)


def solution(mesh):
    return jax.shard_map(
        body,
        mesh=mesh,
        in_specs=(
            P(("sea", "tm"), None),
            P(("sea", "tm"), None),
            P(("sea", "tm")),
            P(("sea", "tm"), None),
            P(),
            P(),
            P(),
            P(),
            P(None, "tm"),
        ),
        out_specs=P("tm", "sea"),
        check_vma=False,
    )
```

```python
import functools

import jax
import jax.numpy as jnp
from jax import lax
from jax.experimental import pallas as pl
from jax.experimental.pallas import tpu as pltpu
from jax.sharding import PartitionSpec as P

F32, BF16, I32 = jnp.float32, jnp.bfloat16, jnp.int32
GIRTH = 500
LANES = 128
HALF = 200
CUT = 104
LEAST = 0.2
CODES = 1023.0
DECADE = 3.3219280948873626
BIAS = 2.0 ** -70


def pow2_up(x, e, bits):
    for b in range(bits):
        x = jnp.where((e & (1 << b)) != 0, x * float(2 ** (1 << b)), x)
    return x


def pow2_down(x, bits):
    e = jnp.zeros(x.shape, I32)
    for b in reversed(range(bits)):
        big = x >= 128.0 * BIAS * 2.0 ** (1 << b)
        x = jnp.where(big, x * float(2.0 ** -(1 << b)), x)
        e = e + jnp.where(big, jnp.int32(1 << b), jnp.int32(0))
    return x * (1.0 / BIAS), e


def shuffled(x, sub):
    x = list(x)
    for k in (1, 2, 4):
        keep = (sub & k) == 0
        for i in range(8):
            if i & k == 0:
                u, v = x[i], x[i | k]
                x[i] = jnp.where(keep, u, pltpu.roll(v, k, 0))
                x[i | k] = jnp.where(keep, pltpu.roll(u, 8 - k, 0), v)
    return x


def forcing_kernel(st_any, gi_any, cnt_any, pr_any, modes_any, word_ref, out_ref,
                   st_ref, gi_ref, cnt_ref, pr_ref, modes_ref, sems, tab, xs, sc, sr, sp,
                   pc, prow, pp, sel1, sel2, fhv, flv, hiv, lov, wt, rankc):
    steps = st_ref.shape[0]
    modes = modes_ref.shape[0]
    blocks = steps // LANES
    copies = [pltpu.make_async_copy(x, y, sems.at[i]) for i, (x, y) in enumerate((
        (cnt_any, cnt_ref), (st_any, st_ref), (gi_any, gi_ref), (pr_any, pr_ref), (modes_any, modes_ref)))]
    for c in copies:
        c.start()
    for h in range(2):
        lanes = slice(LANES * h, LANES * (h + 1))
        word = word_ref[HALF * h:HALF * (h + 1), :]
        first = pow2_up(((word & 127) + 128).astype(F32) * BIAS, ((word >> 7) & 31) + ((word >> 12) & 3) * 32, 7)
        tab[0:HALF, lanes] = jnp.where((word & (4 << 12)) != 0, -first, first).astype(BF16)
        upper = word >> 15
        other = jnp.concatenate([upper[CUT:], jnp.zeros((2 * CUT - HALF, LANES), I32)], axis=0)
        tab[HALF:, lanes] = pow2_up((upper[:CUT] + 128).astype(F32) * BIAS, other, 7).astype(BF16)
    sub = lax.broadcasted_iota(I32, (8, LANES), 0)
    slot = lax.broadcasted_iota(I32, (LANES, LANES), 1).astype(F32)
    line = lax.broadcasted_iota(I32, (LANES, LANES), 0).astype(F32)
    line2 = lax.broadcasted_iota(I32, (2 * LANES, LANES), 0).astype(F32)
    copies[0].wait()
    counts = cnt_ref[...].astype(F32)
    n64 = jnp.sum(jnp.where(counts > 64.0, 1.0, 0.0)).astype(I32)
    n32 = jnp.sum(jnp.where(counts > 32.0, 1.0, 0.0)).astype(I32)
    lane_row = lax.broadcasted_iota(I32, (1, LANES), 1).astype(F32)
    count_row = [counts[j:j + 1, :] for j in range(blocks)]
    key_row = [count_row[j] * float(steps) + (float(steps - 1 - LANES * j) - lane_row) for j in range(blocks)]
    count_col = [jnp.broadcast_to(count_row[j], (LANES, LANES)).T for j in range(blocks)]
    key_col = [count_col[j] * float(steps) + (float(steps - 1 - LANES * j) - line) for j in range(blocks)]
    rank_row = []
    for j in range(blocks):
        above = jnp.zeros((8, LANES), F32)
        for i in range(blocks):
            for v in range(LANES // 8):
                above = above + jnp.where(key_col[i][8 * v:8 * v + 8] > key_row[j], 1.0, 0.0)
        rank_row.append(jnp.sum(above, axis=0, keepdims=True))
        rankc[LANES * j:LANES * (j + 1), :] = jnp.broadcast_to(rank_row[j], (LANES, LANES)).T
    for c in copies[1:4]:
        c.wait()
    for j in range(blocks):
        here = slice(LANES * j, LANES * (j + 1))
        panel = st_ref[here, :] * GIRTH + gi_ref[here, :]
        hi = panel >> 7
        second = hi >= HALF
        xs[here, 0:LANES] = ((panel & 127) + jnp.where(second, LANES, 0)).astype(F32).astype(BF16)
        xs[here, LANES:2 * LANES] = jnp.where(second, hi - HALF, hi).astype(F32).astype(BF16)
        xs[here, 2 * LANES:] = jnp.where(slot < count_col[j], pr_ref[here, :].astype(F32), 0.0).astype(BF16)
    for j in range(blocks // 2):
        here = slice(2 * LANES * j, 2 * LANES * (j + 1))
        place = jnp.concatenate([jnp.where(rank_row[i] == line2 + float(2 * LANES * j), 1.0, 0.0).astype(BF16) for i in range(blocks)], axis=1)
        y = jnp.dot(place, xs[...], preferred_element_type=F32)
        for i, ref in enumerate((sc, sr, sp)):
            ref[here, :] = y[:, LANES * i:LANES * (i + 1)]
    for ref in (sc, sr, sp):
        ref[steps:, :] = jnp.zeros((LANES, LANES), F32)

    group = LANES // 4
    n_full = (n64 + (group - 1)) // group
    base2 = n_full * group
    n_half = (jnp.maximum(n32 - base2, 0) + (2 * group - 1)) // (2 * group)
    left = jnp.maximum(steps - base2 - n_half * 2 * group, 0) // group
    n_full = n_full + jnp.where(left % 4 == 1, 1, 0)
    n_half = n_half + jnp.where(left % 4 == 2, 1, 0)
    base2 = n_full * group
    base4 = base2 + n_half * 2 * group
    n_quarter = (jnp.maximum(steps - base4, 0) + (4 * group - 1)) // (4 * group)
    n_all = n_full + n_half + n_quarter
    firsts = {1: (n_full, 0, 0), 2: (n_half, base2, n_full), 4: (n_quarter, base4, n_full + n_half)}
    lane = lax.broadcasted_iota(I32, (group, LANES), 1)

    for pack, (n, start, where) in firsts.items():
        def gather(g, carry, pack=pack, start=start, where=where):
            source = start + g * (group * pack)
            target = pl.multiple_of((where + g) * group, group)
            for s_ref, p_ref in ((sc, pc), (sr, prow), (sp, pp)):
                x = s_ref[pl.ds(pl.multiple_of(source, group), group), :]
                for c in range(1, pack):
                    y = s_ref[pl.ds(pl.multiple_of(source + group * c, group), group), :]
                    x = jnp.where(lane < LANES // pack * c, x, pltpu.roll(y, LANES // pack * c, 1))
                p_ref[pl.ds(target, group), :] = x
            return carry
        lax.fori_loop(0, n, gather, 0)

    iota_b = lax.broadcasted_iota(I32, (256, LANES), 0).astype(F32).astype(BF16)
    one = jnp.ones((), BF16)
    zero = jnp.zeros((), BF16)

    def onehot(row_f32, depth):
        b = jnp.broadcast_to(row_f32, (depth, LANES)).astype(BF16)
        return jnp.where(iota_b[:depth] == b, one, zero)

    def stage1_pair(t0):
        oh = jnp.concatenate([onehot(pc[pl.ds(t0 + j, 1), :], 256) for j in range(2)], axis=1)
        r = jnp.dot(tab[...], oh, preferred_element_type=F32)
        for j in range(2):
            want = jnp.broadcast_to(prow[pl.ds(t0 + j, 1), :].astype(I32), (8, LANES)) - sub
            a1 = jnp.zeros((8, LANES), F32)
            a2 = jnp.zeros((8, LANES), F32)
            for v in range(HALF // 8):
                hit = want == 8 * v
                a1 = jnp.where(hit, r[8 * v:8 * v + 8, LANES * j:LANES * (j + 1)], a1)
                if 8 * v < CUT:
                    shared = hit | (want == 8 * v + CUT)
                    a2 = jnp.where(shared, r[HALF + 8 * v:HALF + 8 * v + 8, LANES * j:LANES * (j + 1)], a2)
            sel1[pl.ds(t0 + j, 1), :] = jnp.sum(a1, axis=0, keepdims=True)
            sel2[pl.ds(t0 + j, 1), :] = jnp.sum(a2, axis=0, keepdims=True)

    def decode(base, count):
        here = pl.ds(base, count)
        x1 = sel1[here, :]
        x2 = sel2[here, :]
        m1, e1 = pow2_down(jnp.abs(x1), 7)
        m2, e2 = pow2_down(x2, 7)
        upper = jnp.where(prow[here, :] >= float(CUT), e2, m2.astype(I32) - 128)
        code = (upper << 3) + jnp.where(x1 < 0, 4, 0) + (e1 >> 5)
        f = pp[here, :] * (LEAST * jnp.exp2(code.astype(F32) * (DECADE / CODES)))
        high = f.astype(BF16).astype(F32)
        fhv[here, :] = high
        flv[here, :] = f - high
        lov[here, :] = m1 - 128.0
        hiv[here, :] = e1 & 31

    sel1[0:group, :] = jnp.full((group, LANES), 128.0 * BIAS, F32)
    sel2[0:group, :] = jnp.full((group, LANES), 128.0 * BIAS, F32)

    def lookup(g, carry):
        before = pl.multiple_of(jnp.maximum(g - 1, 0) * group, group)
        base = pl.multiple_of(g * group, group)
        for p in range(group // 2):
            stage1_pair(base + 2 * p)
            if p % 4 == 1:
                decode(pl.multiple_of(before + 8 * (p // 4), 8), 8)
        return carry

    def lookup_two(i, carry):
        lookup(2 * i, carry)
        return lookup(2 * i + 1, carry)

    lax.fori_loop(0, n_all // 2, lookup_two, 0)
    lax.fori_loop(n_all // 2 * 2, n_all, lookup, 0)
    decode(pl.multiple_of((n_all - 1) * group, group), group)


    high_parts = wt.shape[0]
    iota_h = lax.broadcasted_iota(I32, (high_parts, LANES), 0)
    chunk_lane = lax.broadcasted_iota(I32, (2 * high_parts, LANES), 1)

    for pack, (n, start, where) in firsts.items():
        def scatter(g, carry, pack=pack, start=start, where=where):
            packed = (where + g) * group
            place = start + g * (group * pack)
            for o in range(group // 8):
                sums = [[None] * 8 for _ in range(pack)]
                for p in range(4):
                    rows = []
                    hots = []
                    for j in range(2):
                        t = pl.ds(packed + 8 * o + 2 * p + j, 1)
                        hots.append(onehot(lov[t, :], LANES))
                        hit = jnp.broadcast_to(hiv[t, :], (high_parts, LANES)) == iota_h
                        high = jnp.where(hit, jnp.broadcast_to(fhv[t, :], (high_parts, LANES)), 0.0)
                        low = jnp.where(hit, jnp.broadcast_to(flv[t, :], (high_parts, LANES)), 0.0)
                        both = jnp.concatenate([high, low], axis=0)
                        for c in range(pack):
                            if pack > 1:
                                width = LANES // pack
                                mine = jnp.where((chunk_lane >= width * c) & (chunk_lane < width * (c + 1)), both, 0.0)
                            else:
                                mine = both
                            mine = mine.astype(BF16)
                            none = jnp.zeros_like(mine)
                            rows.append(jnp.concatenate([mine, none] if j == 0 else [none, mine], axis=1))
                    w = lax.dot_general(jnp.concatenate(rows, axis=0), jnp.concatenate(hots, axis=1),
                                        (((1,), (1,)), ((), ())), preferred_element_type=F32)
                    for j in range(2):
                        for c in range(pack):
                            at = 2 * high_parts * (j * pack + c)
                            sums[c][2 * p + j] = w[at:at + high_parts] + w[at + high_parts:at + 2 * high_parts]
                for c in range(pack):
                    spot = pl.ds(pl.multiple_of(place + group * c + 8 * o, 8), 8)
                    for hb in range(high_parts // 8):
                        for i, x in enumerate(shuffled([y[8 * hb:8 * hb + 8] for y in sums[c]], sub)):
                            wt[8 * hb + i, spot, :] = x
            return carry
        if pack < 4:
            def scatter_two(i, carry):
                scatter(2 * i, carry)
                return scatter(2 * i + 1, carry)

            lax.fori_loop(0, n // 2, scatter_two, 0)
            lax.fori_loop(n // 2 * 2, n, scatter, 0)
        else:
            lax.fori_loop(0, n, scatter, 0)

    copies[4].wait()
    ordered = []
    many = 2 * LANES
    for j in range(steps // many):
        here = slice(many * j, many * (j + 1))
        acc = jnp.zeros((2 * many, modes), F32)
        for h in range(high_parts // 2):
            w = jnp.concatenate([wt[2 * h, here, :], wt[2 * h + 1, here, :]], axis=1)
            wh = w.astype(BF16)
            wl = (w - wh.astype(F32)).astype(BF16)
            acc = acc + lax.dot_general(jnp.concatenate([wh, wl], axis=0), modes_ref[:, 256 * h:256 * h + 256],
                                        (((1,), (1,)), ((), ())), preferred_element_type=F32)
        ordered.append((acc[:many] + acc[many:]).astype(BF16))
    ordered = jnp.concatenate(ordered, axis=0)
    for j in range(blocks):
        here = slice(LANES * j, LANES * (j + 1))
        back = jnp.concatenate([jnp.where(rankc[here, :] == slot + float(LANES * i), 1.0, 0.0).astype(BF16) for i in range(blocks)], axis=1)
        out_ref[here, :] = jnp.dot(back, ordered, preferred_element_type=F32).astype(BF16)


def whole(shape):
    return pl.BlockSpec(shape, lambda i: (0,) * len(shape))


def encoded(panel_area, panel_patch):
    pad = 2 * HALF * LANES - panel_area.shape[0]
    code = jnp.clip((jnp.log2(panel_area * (1.0 / LEAST)) * (CODES / DECADE) + 0.5).astype(I32), 0, int(CODES))
    return jnp.pad(panel_patch + (code << 12), (0, pad)).reshape(2 * HALF, LANES)


def forcing(wet_station, wet_girth, wet_count, pressure, panel_area, panel_patch, patch_modes):
    steps = wet_station.shape[0]
    patches, modes = patch_modes.shape
    words = encoded(panel_area, panel_patch)
    far = (wet_station, wet_girth, wet_count.reshape(steps // LANES, LANES), pressure, patch_modes.T)
    far = tuple(pltpu.with_memory_space_constraint(x, pltpu.HBM) for x in far)
    table = lambda n, t: pltpu.VMEM((n, LANES), t)
    return pl.pallas_call(
        forcing_kernel,
        out_shape=jax.ShapeDtypeStruct((steps, modes), BF16),
        in_specs=[pl.BlockSpec(memory_space=pltpu.HBM)] * 5 + [pl.BlockSpec(memory_space=pltpu.VMEM)],
        out_specs=pl.BlockSpec(memory_space=pltpu.VMEM),
        scratch_shapes=[
            *[pltpu.VMEM(x.shape, x.dtype) for x in far],
            pltpu.SemaphoreType.DMA((5,)),
            pltpu.VMEM((HALF + CUT, 256), BF16),
            pltpu.VMEM((steps, 3 * LANES), BF16),
            *[table(steps + LANES, F32)] * 3,
            *[table(steps, F32)] * 7,
            table(steps, I32), table(steps, F32),
            pltpu.VMEM((patches // LANES, steps + LANES, LANES), F32),
            table(steps, F32),
        ],
        compiler_params=pltpu.CompilerParams(vmem_limit_bytes=24 * 1024 * 1024),
        cost_estimate=pl.CostEstimate(flops=2 * 10 ** 10, bytes_accessed=2 * 10 ** 6, transcendentals=0),
        name="forcing",
    )(*far, words)


def weights_kernel(imp_any, out_ref, imp_ref, sems):
    modes = out_ref.shape[1] // 4
    quarter = imp_ref.shape[1] // 4
    row = lax.broadcasted_iota(I32, (2 * quarter, 2 * quarter), 0)
    col = lax.broadcasted_iota(I32, (2 * quarter, 2 * quarter), 1)
    chunk = imp_ref.shape[0] // 4
    copies = [pltpu.make_async_copy(imp_any.at[pl.ds(chunk * c, chunk), :], imp_ref.at[pl.ds(chunk * c, chunk), :], sems.at[c]) for c in range(4)]
    for c in copies:
        c.start()
    order = jnp.where(((row >> 3) & 1) * quarter + (row >> 4) * 8 + (row & 7) == col, 1.0, 0.0).astype(BF16)

    def turn(i, carry):
        pair = [imp_ref[pl.ds(pl.multiple_of((2 * i + m) * modes, modes), modes), :] for m in range(2)]
        block = jnp.concatenate([jnp.concatenate([x[:, quarter * q:quarter * (q + 1)] for x in pair], axis=1) for q in range(4)], axis=0)
        y = lax.dot_general(order, block, (((1,), (1,)), ((), ())), preferred_element_type=F32).astype(BF16)
        for v in range(quarter // 8):
            out_ref[pl.ds(pl.multiple_of(v * (8 * modes) + 16 * i, 16), 16), :] = y[16 * v:16 * v + 16]
        return carry

    for c in range(4):
        copies[c].wait()
        lax.fori_loop(modes // 8 * c, modes // 8 * (c + 1), turn, 0, unroll=True)


def impulse_weights(impulse):
    lags, modes, _ = impulse.shape
    flat = jnp.transpose(impulse, (1, 2, 0)).reshape(modes * modes, lags)
    return pl.pallas_call(
        weights_kernel,
        out_shape=jax.ShapeDtypeStruct((lags // 4 * modes, 4 * modes), BF16),
        in_specs=[pl.BlockSpec(memory_space=pltpu.HBM)],
        out_specs=pl.BlockSpec(memory_space=pltpu.VMEM),
        scratch_shapes=[pltpu.VMEM(flat.shape, BF16), pltpu.SemaphoreType.DMA((4,))],
        compiler_params=pltpu.CompilerParams(vmem_limit_bytes=12 * 1024 * 1024),
        cost_estimate=pl.CostEstimate(flops=3 * 10 ** 9, bytes_accessed=8 * 10 ** 6, transcendentals=0),
        name="impulse_weights",
    )(pltpu.with_memory_space_constraint(flat, pltpu.HBM))


def products(seq, wts, pair, x8, shifts, acc):
    count, modes = seq.shape
    depth = 16 * modes
    steps = wts.shape[0] // depth
    quarter = 16 * steps
    pair[0:8, :] = jnp.zeros((8, 2 * modes), F32)
    pair[8:, 0:modes] = seq
    pair[0:9, modes:] = jnp.zeros((9, modes), F32)
    pair[9:8 + count, modes:] = seq[:-1]
    for i in range(4):
        x8[:, 2 * modes * i:2 * modes * (i + 1)] = pair[8 - 2 * i:8 - 2 * i + count, :].astype(BF16)
    row = lax.broadcasted_iota(I32, (8 * modes, 8 * modes), 0)
    col = lax.broadcasted_iota(I32, (8 * modes, 8 * modes), 1)
    spread = jnp.where((row & (modes - 1)) * 8 + row // modes == col, 1.0, 0.0).astype(BF16)
    last = jnp.zeros((8, 8 * modes), F32)
    big = 4 * LANES
    for k in range(count // big):
        here = slice(big * k, big * (k + 1))
        y = jnp.dot(x8[here, :], spread, preferred_element_type=F32)
        shifts[here, 0:8 * modes] = y.astype(BF16)
        shifts[here, 8 * modes:] = jnp.concatenate([last, y[:-8]], axis=0).astype(BF16)
        last = y[-8:]
    cut = depth // 2
    halves = [None, None]
    for p in range(steps):
        left = shifts[quarter - 16 * p:count - 16 * p, :]
        for i in range(2):
            part = jnp.dot(left[:, cut * i:cut * (i + 1)], wts[depth * p + cut * i:depth * p + cut * (i + 1), :], preferred_element_type=F32)
            halves[i] = part if p == 0 else halves[i] + part
    acc[...] = halves[0] + halves[1]


def stress_kernel(early_ref, force_ref, map_ref, wts, out_ref, pair, x8, shifts, acc):
    steps, modes = force_ref.shape
    quarter = wts.shape[0] // modes
    seq = jnp.concatenate([early_ref[...], force_ref[...]], axis=0).astype(F32)
    products(seq, wts, pair, x8, shifts, acc)

    def y(q):
        return acc[(3 - q) * quarter:(3 - q) * quarter + steps, 128 * (q // 2):128 * (q // 2) + 128]

    lane = lax.broadcasted_iota(I32, (steps, 2 * modes), 1) < modes
    s = jnp.where(lane, y(0), y(1)) + jnp.where(lane, y(2), y(3))
    response = (s[:, :modes] + s[:, modes:]).astype(BF16)
    hot_map = map_ref[...].reshape(-1, 2 * modes)[:, :modes]
    out_ref[...] = lax.dot_general(hot_map, response, (((1,), (1,)), ((), ())), preferred_element_type=F32).astype(BF16)


def work(count, modes):
    return [
        pltpu.VMEM((count + 8, 2 * modes), F32),
        pltpu.VMEM((count, 8 * modes), BF16),
        pltpu.VMEM((count, 16 * modes), BF16),
    ]


def local_stress(early, force, whole_map, weights):
    steps, modes = force.shape
    quarter = weights.shape[0] // modes
    hot = whole_map.shape[0] * whole_map.shape[1]
    return pl.pallas_call(
        stress_kernel,
        out_shape=jax.ShapeDtypeStruct((hot, steps), BF16),
        in_specs=[pl.BlockSpec(memory_space=pltpu.VMEM)] * 4,
        out_specs=pl.BlockSpec(memory_space=pltpu.VMEM),
        scratch_shapes=[*work(2 * steps, modes), pltpu.VMEM((2 * steps - quarter, 4 * modes), F32)],
        compiler_params=pltpu.CompilerParams(vmem_limit_bytes=20480 * 1024),
        cost_estimate=pl.CostEstimate(flops=4 * 10 ** 9, bytes_accessed=5 * 10 ** 6, transcendentals=0),
        name="local_stress",
    )(early, force, whole_map, weights)


def shifted(value, axis, steps):
    count = lax.axis_size(axis)
    leading, last = (max(0, -steps), min(count, count - steps))
    return lax.ppermute(value, axis, [(source, source + steps) for source in range(leading, last)])


def body(wet_station, wet_girth, wet_count, pressure, panel_area, panel_patch, patch_modes, impulse, stress_map):
    steps = wet_station.shape[0]
    hot, modes = stress_map.shape[1], stress_map.shape[0]
    own_map = jnp.broadcast_to(jnp.pad(stress_map.T, ((0, 0), (0, modes)))[None], (lax.axis_size("tm"), hot, 2 * modes))
    whole_map = lax.all_to_all(own_map, "tm", 0, 0, tiled=True)
    force = forcing(wet_station, wet_girth, wet_count, pressure, panel_area, panel_patch, patch_modes)
    force, whole_map = lax.optimization_barrier((force, whole_map))
    early = shifted(force, "tm", 1)
    weights = pltpu.with_memory_space_constraint(impulse_weights(impulse), pltpu.VMEM)
    part = local_stress(early, force, whole_map, weights)
    return lax.all_to_all(part, "tm", 0, 1, tiled=True)


def solution(mesh):
    return jax.shard_map(
        body,
        mesh=mesh,
        in_specs=(
            P(("sea", "tm"), None),
            P(("sea", "tm"), None),
            P(("sea", "tm")),
            P(("sea", "tm"), None),
            P(),
            P(),
            P(),
            P(),
            P(None, "tm"),
        ),
        out_specs=P("tm", "sea"),
        check_vma=False,
    )
```

```python
import functools

import jax
import jax.numpy as jnp
from jax import lax
from jax.experimental import pallas as pl
from jax.experimental.pallas import tpu as pltpu
from jax.sharding import PartitionSpec as P

F32, BF16, I32 = jnp.float32, jnp.bfloat16, jnp.int32
GIRTH = 500
LANES = 128
HALF = 200
CUT = 104
LEAST = 0.2
CODES = 1023.0
DECADE = 3.3219280948873626
BIAS = 2.0 ** -70


def pow2_up(x, e, bits):
    for b in range(bits):
        x = jnp.where((e & (1 << b)) != 0, x * float(2 ** (1 << b)), x)
    return x


def pow2_down(x, bits):
    e = jnp.zeros(x.shape, I32)
    for b in reversed(range(bits)):
        big = x >= 128.0 * BIAS * 2.0 ** (1 << b)
        x = jnp.where(big, x * float(2.0 ** -(1 << b)), x)
        e = e + jnp.where(big, jnp.int32(1 << b), jnp.int32(0))
    return x * (1.0 / BIAS), e


def shuffled(x, sub):
    x = list(x)
    for k in (1, 2, 4):
        keep = (sub & k) == 0
        for i in range(8):
            if i & k == 0:
                u, v = x[i], x[i | k]
                x[i] = jnp.where(keep, u, pltpu.roll(v, k, 0))
                x[i | k] = jnp.where(keep, pltpu.roll(u, 8 - k, 0), v)
    return x


def forcing_kernel(st_any, gi_any, cnt_any, pr_any, modes_any, word_ref, out_ref,
                   st_ref, gi_ref, cnt_ref, pr_ref, modes_ref, sems, tab, xs, sc, sr, sp,
                   pc, prow, pp, sel1, sel2, fhv, flv, hiv, lov, wt, rankc):
    steps = st_ref.shape[0]
    modes = modes_ref.shape[0]
    blocks = steps // LANES
    copies = [pltpu.make_async_copy(x, y, sems.at[i]) for i, (x, y) in enumerate((
        (cnt_any, cnt_ref), (st_any, st_ref), (gi_any, gi_ref), (pr_any, pr_ref), (modes_any, modes_ref)))]
    for c in copies:
        c.start()
    for h in range(2):
        lanes = slice(LANES * h, LANES * (h + 1))
        word = word_ref[HALF * h:HALF * (h + 1), :]
        first = pow2_up(((word & 127) + 128).astype(F32) * BIAS, ((word >> 7) & 31) + ((word >> 12) & 3) * 32, 7)
        tab[0:HALF, lanes] = jnp.where((word & (4 << 12)) != 0, -first, first).astype(BF16)
        upper = word >> 15
        other = jnp.concatenate([upper[CUT:], jnp.zeros((2 * CUT - HALF, LANES), I32)], axis=0)
        tab[HALF:, lanes] = pow2_up((upper[:CUT] + 128).astype(F32) * BIAS, other, 7).astype(BF16)
    sub = lax.broadcasted_iota(I32, (8, LANES), 0)
    slot = lax.broadcasted_iota(I32, (LANES, LANES), 1).astype(F32)
    line = lax.broadcasted_iota(I32, (LANES, LANES), 0).astype(F32)
    line2 = lax.broadcasted_iota(I32, (2 * LANES, LANES), 0).astype(F32)
    copies[0].wait()
    counts = cnt_ref[...].astype(F32)
    n64 = jnp.sum(jnp.where(counts > 64.0, 1.0, 0.0)).astype(I32)
    n32 = jnp.sum(jnp.where(counts > 32.0, 1.0, 0.0)).astype(I32)
    lane_row = lax.broadcasted_iota(I32, (1, LANES), 1).astype(F32)
    count_row = [counts[j:j + 1, :] for j in range(blocks)]
    key_row = [count_row[j] * float(steps) + (float(steps - 1 - LANES * j) - lane_row) for j in range(blocks)]
    count_col = [jnp.broadcast_to(count_row[j], (LANES, LANES)).T for j in range(blocks)]
    key_col = [count_col[j] * float(steps) + (float(steps - 1 - LANES * j) - line) for j in range(blocks)]
    rank_row = []
    for j in range(blocks):
        above = jnp.zeros((8, LANES), F32)
        for i in range(blocks):
            for v in range(LANES // 8):
                above = above + jnp.where(key_col[i][8 * v:8 * v + 8] > key_row[j], 1.0, 0.0)
        rank_row.append(jnp.sum(above, axis=0, keepdims=True))
        rankc[LANES * j:LANES * (j + 1), :] = jnp.broadcast_to(rank_row[j], (LANES, LANES)).T
    for c in copies[1:4]:
        c.wait()
    for j in range(blocks):
        here = slice(LANES * j, LANES * (j + 1))
        panel = st_ref[here, :] * GIRTH + gi_ref[here, :]
        hi = panel >> 7
        second = hi >= HALF
        xs[here, 0:LANES] = ((panel & 127) + jnp.where(second, LANES, 0)).astype(F32).astype(BF16)
        xs[here, LANES:2 * LANES] = jnp.where(second, hi - HALF, hi).astype(F32).astype(BF16)
        xs[here, 2 * LANES:] = jnp.where(slot < count_col[j], pr_ref[here, :].astype(F32), 0.0).astype(BF16)
    for j in range(blocks // 2):
        here = slice(2 * LANES * j, 2 * LANES * (j + 1))
        place = jnp.concatenate([jnp.where(rank_row[i] == line2 + float(2 * LANES * j), 1.0, 0.0).astype(BF16) for i in range(blocks)], axis=1)
        y = jnp.dot(place, xs[...], preferred_element_type=F32)
        for i, ref in enumerate((sc, sr, sp)):
            ref[here, :] = y[:, LANES * i:LANES * (i + 1)]
    for ref in (sc, sr, sp):
        ref[steps:, :] = jnp.zeros((LANES, LANES), F32)

    group = LANES // 4
    n_full = (n64 + (group - 1)) // group
    base2 = n_full * group
    n_half = (jnp.maximum(n32 - base2, 0) + (2 * group - 1)) // (2 * group)
    left = jnp.maximum(steps - base2 - n_half * 2 * group, 0) // group
    n_full = n_full + jnp.where(left % 4 == 1, 1, 0)
    n_half = n_half + jnp.where(left % 4 == 2, 1, 0)
    base2 = n_full * group
    base4 = base2 + n_half * 2 * group
    n_quarter = (jnp.maximum(steps - base4, 0) + (4 * group - 1)) // (4 * group)
    n_all = n_full + n_half + n_quarter
    firsts = {1: (n_full, 0, 0), 2: (n_half, base2, n_full), 4: (n_quarter, base4, n_full + n_half)}
    lane = lax.broadcasted_iota(I32, (group, LANES), 1)

    for pack, (n, start, where) in firsts.items():
        def gather(g, carry, pack=pack, start=start, where=where):
            source = start + g * (group * pack)
            target = pl.multiple_of((where + g) * group, group)
            for s_ref, p_ref in ((sc, pc), (sr, prow), (sp, pp)):
                x = s_ref[pl.ds(pl.multiple_of(source, group), group), :]
                for c in range(1, pack):
                    y = s_ref[pl.ds(pl.multiple_of(source + group * c, group), group), :]
                    x = jnp.where(lane < LANES // pack * c, x, pltpu.roll(y, LANES // pack * c, 1))
                p_ref[pl.ds(target, group), :] = x
            return carry
        lax.fori_loop(0, n, gather, 0)

    iota_b = lax.broadcasted_iota(I32, (256, LANES), 0).astype(F32).astype(BF16)
    one = jnp.ones((), BF16)
    zero = jnp.zeros((), BF16)

    def onehot(row_f32, depth):
        b = jnp.broadcast_to(row_f32, (depth, LANES)).astype(BF16)
        return jnp.where(iota_b[:depth] == b, one, zero)

    def stage1_pair(t0):
        oh = jnp.concatenate([onehot(pc[pl.ds(t0 + j, 1), :], 256) for j in range(2)], axis=1)
        r = jnp.dot(tab[...], oh, preferred_element_type=F32)
        for j in range(2):
            want = jnp.broadcast_to(prow[pl.ds(t0 + j, 1), :].astype(I32), (8, LANES)) - sub
            a1 = jnp.zeros((8, LANES), F32)
            a2 = jnp.zeros((8, LANES), F32)
            for v in range(HALF // 8):
                hit = want == 8 * v
                a1 = jnp.where(hit, r[8 * v:8 * v + 8, LANES * j:LANES * (j + 1)], a1)
                if 8 * v < CUT:
                    shared = hit | (want == 8 * v + CUT)
                    a2 = jnp.where(shared, r[HALF + 8 * v:HALF + 8 * v + 8, LANES * j:LANES * (j + 1)], a2)
            sel1[pl.ds(t0 + j, 1), :] = jnp.sum(a1, axis=0, keepdims=True)
            sel2[pl.ds(t0 + j, 1), :] = jnp.sum(a2, axis=0, keepdims=True)

    def decode(base, count):
        here = pl.ds(base, count)
        x1 = sel1[here, :]
        x2 = sel2[here, :]
        m1, e1 = pow2_down(jnp.abs(x1), 7)
        m2, e2 = pow2_down(x2, 7)
        upper = jnp.where(prow[here, :] >= float(CUT), e2, m2.astype(I32) - 128)
        code = (upper << 3) + jnp.where(x1 < 0, 4, 0) + (e1 >> 5)
        f = pp[here, :] * (LEAST * jnp.exp2(code.astype(F32) * (DECADE / CODES)))
        high = f.astype(BF16).astype(F32)
        fhv[here, :] = high
        flv[here, :] = f - high
        lov[here, :] = m1 - 128.0
        hiv[here, :] = e1 & 31

    sel1[0:group, :] = jnp.full((group, LANES), 128.0 * BIAS, F32)
    sel2[0:group, :] = jnp.full((group, LANES), 128.0 * BIAS, F32)

    def lookup(g, carry):
        before = pl.multiple_of(jnp.maximum(g - 1, 0) * group, group)
        base = pl.multiple_of(g * group, group)
        for p in range(group // 2):
            stage1_pair(base + 2 * p)
            if p % 4 == 1:
                decode(pl.multiple_of(before + 8 * (p // 4), 8), 8)
        return carry

    def lookup_two(i, carry):
        lookup(2 * i, carry)
        return lookup(2 * i + 1, carry)

    lax.fori_loop(0, n_all // 2, lookup_two, 0)
    lax.fori_loop(n_all // 2 * 2, n_all, lookup, 0)
    decode(pl.multiple_of((n_all - 1) * group, group), group)


    high_parts = wt.shape[0]
    iota_h = lax.broadcasted_iota(I32, (high_parts, LANES), 0)
    chunk_lane = lax.broadcasted_iota(I32, (2 * high_parts, LANES), 1)

    for pack, (n, start, where) in firsts.items():
        def scatter(g, carry, pack=pack, start=start, where=where):
            packed = (where + g) * group
            place = start + g * (group * pack)
            for o in range(group // 8):
                sums = [[None] * 8 for _ in range(pack)]
                for p in range(4):
                    rows = []
                    hots = []
                    for j in range(2):
                        t = pl.ds(packed + 8 * o + 2 * p + j, 1)
                        hots.append(onehot(lov[t, :], LANES))
                        hit = jnp.broadcast_to(hiv[t, :], (high_parts, LANES)) == iota_h
                        high = jnp.where(hit, jnp.broadcast_to(fhv[t, :], (high_parts, LANES)), 0.0)
                        low = jnp.where(hit, jnp.broadcast_to(flv[t, :], (high_parts, LANES)), 0.0)
                        both = jnp.concatenate([high, low], axis=0)
                        for c in range(pack):
                            if pack > 1:
                                width = LANES // pack
                                mine = jnp.where((chunk_lane >= width * c) & (chunk_lane < width * (c + 1)), both, 0.0)
                            else:
                                mine = both
                            mine = mine.astype(BF16)
                            none = jnp.zeros_like(mine)
                            rows.append(jnp.concatenate([mine, none] if j == 0 else [none, mine], axis=1))
                    w = lax.dot_general(jnp.concatenate(rows, axis=0), jnp.concatenate(hots, axis=1),
                                        (((1,), (1,)), ((), ())), preferred_element_type=F32)
                    for j in range(2):
                        for c in range(pack):
                            at = 2 * high_parts * (j * pack + c)
                            sums[c][2 * p + j] = w[at:at + high_parts] + w[at + high_parts:at + 2 * high_parts]
                for c in range(pack):
                    spot = pl.ds(pl.multiple_of(place + group * c + 8 * o, 8), 8)
                    for hb in range(high_parts // 8):
                        for i, x in enumerate(shuffled([y[8 * hb:8 * hb + 8] for y in sums[c]], sub)):
                            wt[8 * hb + i, spot, :] = x
            return carry
        if pack < 4:
            def scatter_two(i, carry):
                scatter(2 * i, carry)
                return scatter(2 * i + 1, carry)

            lax.fori_loop(0, n // 2, scatter_two, 0)
            lax.fori_loop(n // 2 * 2, n, scatter, 0)
        else:
            lax.fori_loop(0, n, scatter, 0)

    copies[4].wait()
    ordered = []
    many = 2 * LANES
    for j in range(steps // many):
        here = slice(many * j, many * (j + 1))
        acc = jnp.zeros((2 * many, modes), F32)
        for h in range(high_parts // 2):
            w = jnp.concatenate([wt[2 * h, here, :], wt[2 * h + 1, here, :]], axis=1)
            wh = w.astype(BF16)
            wl = (w - wh.astype(F32)).astype(BF16)
            acc = acc + lax.dot_general(jnp.concatenate([wh, wl], axis=0), modes_ref[:, 256 * h:256 * h + 256],
                                        (((1,), (1,)), ((), ())), preferred_element_type=F32)
        ordered.append((acc[:many] + acc[many:]).astype(BF16))
    ordered = jnp.concatenate(ordered, axis=0)
    for j in range(blocks):
        here = slice(LANES * j, LANES * (j + 1))
        back = jnp.concatenate([jnp.where(rankc[here, :] == slot + float(LANES * i), 1.0, 0.0).astype(BF16) for i in range(blocks)], axis=1)
        out_ref[here, :] = jnp.dot(back, ordered, preferred_element_type=F32).astype(BF16)


def whole(shape):
    return pl.BlockSpec(shape, lambda i: (0,) * len(shape))


def encoded(panel_area, panel_patch):
    pad = 2 * HALF * LANES - panel_area.shape[0]
    code = jnp.clip((jnp.log2(panel_area * (1.0 / LEAST)) * (CODES / DECADE) + 0.5).astype(I32), 0, int(CODES))
    return jnp.pad(panel_patch + (code << 12), (0, pad)).reshape(2 * HALF, LANES)


def forcing(wet_station, wet_girth, wet_count, pressure, panel_area, panel_patch, patch_modes):
    steps = wet_station.shape[0]
    patches, modes = patch_modes.shape
    words = encoded(panel_area, panel_patch)
    far = (wet_station, wet_girth, wet_count.reshape(steps // LANES, LANES), pressure, patch_modes.T)
    far = tuple(pltpu.with_memory_space_constraint(x, pltpu.HBM) for x in far)
    table = lambda n, t: pltpu.VMEM((n, LANES), t)
    return pl.pallas_call(
        forcing_kernel,
        out_shape=jax.ShapeDtypeStruct((steps, modes), BF16),
        in_specs=[pl.BlockSpec(memory_space=pltpu.HBM)] * 5 + [pl.BlockSpec(memory_space=pltpu.VMEM)],
        out_specs=pl.BlockSpec(memory_space=pltpu.VMEM),
        scratch_shapes=[
            *[pltpu.VMEM(x.shape, x.dtype) for x in far],
            pltpu.SemaphoreType.DMA((5,)),
            pltpu.VMEM((HALF + CUT, 256), BF16),
            pltpu.VMEM((steps, 3 * LANES), BF16),
            *[table(steps + LANES, F32)] * 3,
            *[table(steps, F32)] * 7,
            table(steps, I32), table(steps, F32),
            pltpu.VMEM((patches // LANES, steps + LANES, LANES), F32),
            table(steps, F32),
        ],
        compiler_params=pltpu.CompilerParams(vmem_limit_bytes=24 * 1024 * 1024),
        cost_estimate=pl.CostEstimate(flops=2 * 10 ** 10, bytes_accessed=2 * 10 ** 6, transcendentals=0),
        name="forcing",
    )(*far, words)


def weights_kernel(imp_any, out_ref, imp_ref, sems):
    modes = out_ref.shape[1] // 4
    quarter = imp_ref.shape[1] // 4
    row = lax.broadcasted_iota(I32, (2 * quarter, 2 * quarter), 0)
    col = lax.broadcasted_iota(I32, (2 * quarter, 2 * quarter), 1)
    chunk = imp_ref.shape[0] // 2
    copies = [pltpu.make_async_copy(imp_any.at[pl.ds(chunk * c, chunk), :], imp_ref.at[pl.ds(chunk * c, chunk), :], sems.at[c]) for c in range(2)]
    for c in copies:
        c.start()
    order = jnp.where(((row >> 3) & 1) * quarter + (row >> 4) * 8 + (row & 7) == col, 1.0, 0.0).astype(BF16)

    def turn(i, carry):
        pair = [imp_ref[pl.ds(pl.multiple_of((2 * i + m) * modes, modes), modes), :] for m in range(2)]
        block = jnp.concatenate([jnp.concatenate([x[:, quarter * q:quarter * (q + 1)] for x in pair], axis=1) for q in range(4)], axis=0)
        y = lax.dot_general(order, block, (((1,), (1,)), ((), ())), preferred_element_type=F32).astype(BF16)
        for v in range(quarter // 8):
            out_ref[pl.ds(pl.multiple_of(v * (8 * modes) + 16 * i, 16), 16), :] = y[16 * v:16 * v + 16]
        return carry

    for c in range(2):
        copies[c].wait()
        lax.fori_loop(modes // 4 * c, modes // 4 * (c + 1), turn, 0, unroll=True)


def impulse_weights(impulse):
    lags, modes, _ = impulse.shape
    flat = jnp.transpose(impulse, (1, 2, 0)).reshape(modes * modes, lags)
    return pl.pallas_call(
        weights_kernel,
        out_shape=jax.ShapeDtypeStruct((lags // 4 * modes, 4 * modes), BF16),
        in_specs=[pl.BlockSpec(memory_space=pltpu.HBM)],
        out_specs=pl.BlockSpec(memory_space=pltpu.VMEM),
        scratch_shapes=[pltpu.VMEM(flat.shape, BF16), pltpu.SemaphoreType.DMA((2,))],
        compiler_params=pltpu.CompilerParams(vmem_limit_bytes=12 * 1024 * 1024),
        cost_estimate=pl.CostEstimate(flops=3 * 10 ** 9, bytes_accessed=8 * 10 ** 6, transcendentals=0),
        name="impulse_weights",
    )(pltpu.with_memory_space_constraint(flat, pltpu.HBM))


def products(seq, wts, pair, x8, shifts, acc):
    count, modes = seq.shape
    depth = 16 * modes
    steps = wts.shape[0] // depth
    quarter = 16 * steps
    pair[0:8, :] = jnp.zeros((8, 2 * modes), F32)
    pair[8:, 0:modes] = seq
    pair[0:9, modes:] = jnp.zeros((9, modes), F32)
    pair[9:8 + count, modes:] = seq[:-1]
    for i in range(4):
        x8[:, 2 * modes * i:2 * modes * (i + 1)] = pair[8 - 2 * i:8 - 2 * i + count, :].astype(BF16)
    row = lax.broadcasted_iota(I32, (8 * modes, 8 * modes), 0)
    col = lax.broadcasted_iota(I32, (8 * modes, 8 * modes), 1)
    spread = jnp.where((row & (modes - 1)) * 8 + row // modes == col, 1.0, 0.0).astype(BF16)
    last = jnp.zeros((8, 8 * modes), F32)
    big = count
    for k in range(count // big):
        here = slice(big * k, big * (k + 1))
        y = jnp.dot(x8[here, :], spread, preferred_element_type=F32)
        shifts[here, 0:8 * modes] = y.astype(BF16)
        shifts[here, 8 * modes:] = jnp.concatenate([last, y[:-8]], axis=0).astype(BF16)
        last = y[-8:]
    cut = depth // 2
    halves = [None, None]
    for p in range(steps):
        left = shifts[quarter - 16 * p:count - 16 * p, :]
        for i in range(2):
            part = jnp.dot(left[:, cut * i:cut * (i + 1)], wts[depth * p + cut * i:depth * p + cut * (i + 1), :], preferred_element_type=F32)
            halves[i] = part if p == 0 else halves[i] + part
    acc[...] = halves[0] + halves[1]


def stress_kernel(early_ref, force_ref, map_ref, wts, out_ref, pair, x8, shifts, acc):
    steps, modes = force_ref.shape
    quarter = wts.shape[0] // modes
    seq = jnp.concatenate([early_ref[...], force_ref[...]], axis=0).astype(F32)
    products(seq, wts, pair, x8, shifts, acc)

    def y(q):
        return acc[(3 - q) * quarter:(3 - q) * quarter + steps, 128 * (q // 2):128 * (q // 2) + 128]

    lane = lax.broadcasted_iota(I32, (steps, 2 * modes), 1) < modes
    s = jnp.where(lane, y(0), y(1)) + jnp.where(lane, y(2), y(3))
    response = (s[:, :modes] + s[:, modes:]).astype(BF16)
    hot_map = map_ref[...].reshape(-1, 2 * modes)[:, :modes]
    out_ref[...] = lax.dot_general(hot_map, response, (((1,), (1,)), ((), ())), preferred_element_type=F32).astype(BF16)


def work(count, modes):
    return [
        pltpu.VMEM((count + 8, 2 * modes), F32),
        pltpu.VMEM((count, 8 * modes), BF16),
        pltpu.VMEM((count, 16 * modes), BF16),
    ]


def local_stress(early, force, whole_map, weights):
    steps, modes = force.shape
    quarter = weights.shape[0] // modes
    hot = whole_map.shape[0] * whole_map.shape[1]
    return pl.pallas_call(
        stress_kernel,
        out_shape=jax.ShapeDtypeStruct((hot, steps), BF16),
        in_specs=[pl.BlockSpec(memory_space=pltpu.VMEM)] * 4,
        out_specs=pl.BlockSpec(memory_space=pltpu.VMEM),
        scratch_shapes=[*work(2 * steps, modes), pltpu.VMEM((2 * steps - quarter, 4 * modes), F32)],
        compiler_params=pltpu.CompilerParams(vmem_limit_bytes=20480 * 1024),
        cost_estimate=pl.CostEstimate(flops=4 * 10 ** 9, bytes_accessed=5 * 10 ** 6, transcendentals=0),
        name="local_stress",
    )(early, force, whole_map, weights)


def shifted(value, axis, steps):
    count = lax.axis_size(axis)
    leading, last = (max(0, -steps), min(count, count - steps))
    return lax.ppermute(value, axis, [(source, source + steps) for source in range(leading, last)])


def body(wet_station, wet_girth, wet_count, pressure, panel_area, panel_patch, patch_modes, impulse, stress_map):
    steps = wet_station.shape[0]
    hot, modes = stress_map.shape[1], stress_map.shape[0]
    own_map = jnp.broadcast_to(jnp.pad(stress_map.T, ((0, 0), (0, modes)))[None], (lax.axis_size("tm"), hot, 2 * modes))
    whole_map = lax.all_to_all(own_map, "tm", 0, 0, tiled=True)
    force = forcing(wet_station, wet_girth, wet_count, pressure, panel_area, panel_patch, patch_modes)
    force, whole_map = lax.optimization_barrier((force, whole_map))
    early = shifted(force, "tm", 1)
    weights = pltpu.with_memory_space_constraint(impulse_weights(impulse), pltpu.VMEM)
    part = local_stress(early, force, whole_map, weights)
    return lax.all_to_all(part, "tm", 0, 1, tiled=True)


def solution(mesh):
    return jax.shard_map(
        body,
        mesh=mesh,
        in_specs=(
            P(("sea", "tm"), None),
            P(("sea", "tm"), None),
            P(("sea", "tm")),
            P(("sea", "tm"), None),
            P(),
            P(),
            P(),
            P(),
            P(None, "tm"),
        ),
        out_specs=P("tm", "sea"),
        check_vma=False,
    )
```
